256 devices in a mesh: rep: 8 (over z), exp: 32 (over y, x, core).
Axes of the slice: x: 4, y: 4, z: 8, core: 2. Of those that a mesh axis runs over, the one named last changes fastest.
Arguments:
- tokens: bfloat16 [16384, 7168], P(('rep', 'exp')), may hold values from -6 to 6
- expert_ids: int32 [16384, 2], P(('rep', 'exp')), may hold values from 0 to 31, as said below
- combine_weights: bfloat16 [16384, 2], P(('rep', 'exp')), may hold values from 0.19921875 to 1
- gate_up_weight: bfloat16 [32, 7168, 2, 1024], P('exp', 'rep'), may hold values from -0.0625 to 0.0625
- down_weight: bfloat16 [32, 1024, 7168], P('exp', None, 'rep'), may hold values from -0.1875 to 0.1875
Outputs:
- combined: float32 [16384, 7168], P(('rep', 'exp'))
- hessian: float32 [32, 1024, 1024], P('exp', 'rep')
The draws below stay inside these ranges and needn't reach their ends.
Inputs may be any that keep to these rules, and one draw needn't show every extreme that they name: `expert_ids`: the 2 experts of a token differ. Among the 64 rows of one device no expert is named by more than 4 rows, and on every device some expert is named exactly 4 times.
All inputs are finite; a program needn't handle non-finite values.
Results may differ from the reference program's by a relative error of at most 0.0041.
Values may be sent and summed in bfloat16 or wider, within the bound.
A program may use at most 64 MiB of HBM per device.

```python
import jax
import jax.numpy as jnp
from jax import lax

D = 7168
FF = 1024
TOP = 2
TOK_DEV = 64
WIN = 32
CAP = 4
TOKENS = 16384
N_REP = 8
N_EXP = 32


def routed_block(block_key):
    group = WIN // TOP
    slots = group * CAP
    excess = slots - TOK_DEV
    columns = []
    for column in range(TOP):
        own = jax.random.fold_in(block_key, column)
        drop_rank = jax.random.permutation(jax.random.fold_in(own, 1), slots - CAP).astype(jnp.int32)
        keep = jnp.concatenate([jnp.ones((CAP,), jnp.int32), (drop_rank >= excess).astype(jnp.int32)])
        sort_key = (1 - keep) * slots + jnp.arange(slots, dtype=jnp.int32)
        kept = jnp.argsort(sort_key).astype(jnp.int32)
        labels = kept[:TOK_DEV] // CAP + column * group
        shuffle = jax.random.permutation(jax.random.fold_in(own, 2), TOK_DEV).astype(jnp.int32)
        columns.append(labels[shuffle])
    table = jnp.stack(columns, axis=1).astype(jnp.int32)
    relabel = jax.random.permutation(jax.random.fold_in(block_key, TOP + 7), WIN).astype(jnp.int32)
    return relabel[table]


def draw_expert_ids(key, part):
    key = jax.random.fold_in(key, 11)
    block_keys = jax.random.split(key, TOKENS // TOK_DEV)
    blocks = jax.vmap(routed_block)(block_keys)
    return blocks.reshape(TOKENS, TOP).astype(jnp.int32)


def shard_levels(key, extent, shards, low, high):
    def one(dim, blocks):
        steps = jax.random.uniform(jax.random.fold_in(jax.random.fold_in(key, 6), dim), (blocks,), jnp.float32, low / len(shards), high / len(shards))
        return jnp.repeat(jnp.exp(steps), extent[dim] // blocks).reshape((-1,) + (1,) * (len(extent) - dim - 1))

    loudness = one(*shards[0])
    for cut in shards[1:]:
        loudness = loudness * one(*cut)
    return loudness


def centred(own_key, extent, deviation, limit, shards=(), kind=jnp.bfloat16):
    entries = deviation * jax.random.normal(own_key, extent, jnp.float32)
    if shards:
        entries = entries * shard_levels(own_key, extent, shards, -0.22, 0.18)
    return jnp.clip(entries, -limit, limit).astype(kind)


def setup_inputs(seed: int = 0) -> dict:
    keys = jax.random.split(jax.random.key(seed), 6)
    tokens = centred(keys[0], (TOKENS, D), 1.0, 6.0, ((0, 256),))
    expert_ids = draw_expert_ids(jax.random.fold_in(keys[5], 71), 0)
    combine_weights = jnp.clip(0.19921875 + 0.80078125 * jax.random.uniform(keys[2], (TOKENS, TOP), jnp.float32) ** shard_levels(keys[2], (TOKENS, TOP), ((0, 256),), -0.2, 0.2), 0.19921875, 1.0).astype(jnp.bfloat16)
    gate_up_weight = centred(keys[3], (WIN, D, 2, FF), D ** -0.5, 0.0625, ((0, 32), (1, 8)))
    down_weight = centred(keys[4], (WIN, FF, D), FF ** -0.5, 0.1875, ((0, 32), (2, 8)))
    return {"tokens": tokens, "expert_ids": expert_ids, "combine_weights": combine_weights, "gate_up_weight": gate_up_weight, "down_weight": down_weight}


def reference(tokens, expert_ids, combine_weights, gate_up_weight, down_weight):
    most_rows = N_REP * N_EXP * CAP
    scale = 2.0 / most_rows
    flat = expert_ids.reshape(-1).astype(jnp.int32)
    routes = flat.shape[0]
    order = jnp.argsort(flat, stable=True).astype(jnp.int32)
    counts = jnp.sum((flat[:, None] == jnp.arange(WIN, dtype=jnp.int32)[None, :]).astype(jnp.int32), axis=0)
    starts = (jnp.cumsum(counts) - counts).astype(jnp.int32)
    padded = jnp.concatenate([order, jnp.zeros((most_rows,), jnp.int32)])

    def one_expert(expert):
        index_rows = lax.dynamic_slice_in_dim(padded, starts[expert], most_rows)
        valid = jnp.arange(most_rows, dtype=jnp.int32) < counts[expert]
        picked = tokens[index_rows // TOP]
        rows = jnp.where(valid[:, None], picked, jnp.zeros_like(picked))
        weights = gate_up_weight[expert].reshape(D, 2 * FF)
        pre = jnp.dot(rows, weights, preferred_element_type=jnp.float32)
        hidden = (jax.nn.silu(pre[:, :FF]) * pre[:, FF:]).astype(jnp.bfloat16)
        hess = scale * jnp.dot(hidden.T, hidden, preferred_element_type=jnp.float32)
        result = jnp.dot(hidden, down_weight[expert], preferred_element_type=jnp.float32).astype(jnp.bfloat16)
        return hess, result

    hessian, outputs = lax.map(one_expert, jnp.arange(WIN, dtype=jnp.int32))
    position = jnp.zeros((routes,), jnp.int32).at[order].set(jnp.arange(routes, dtype=jnp.int32))
    rank = (position - starts[flat]).reshape(TOKENS, TOP)
    total = jnp.zeros((TOKENS, D), jnp.float32)
    for slot in range(TOP):
        chosen = outputs[expert_ids[:, slot], rank[:, slot]].astype(jnp.float32)
        total = total + combine_weights[:, slot].astype(jnp.float32)[:, None] * chosen
    return total, hessian
```

```python
import functools

import jax
import jax.numpy as jnp
from jax import lax
from jax.experimental import pallas as pl
from jax.experimental.pallas import tpu as pltpu
from jax.sharding import PartitionSpec as P

MESH = pl.DeviceIdType.MESH
Z = 8
E = 32
TOK = 64
SLOT = 4
D = 7168
DS = D // Z
FF = 1024
ROWS = 512
BLK = 16
CH = ROWS // Z
NSUB = 2
SUB = CH // NSUB
MSG = 2 * FF + 128
LEVELS = 32000.0
FAR = ((4, 3), (3, 4))


def kernel(
    tok, meta, w3, dn, comb_out, hess_out,
    T, M, DM, CT, G, X, W3V, W, DN, PRE, RSS, RSR, HD, OUT, B, CB,
    loc, p1s, p1r, m1s, m1r, p3s, p3r, rss, rsr, ags, agr, p8s, p8r, p10s, p10r,
):
    r = lax.axis_index("rep")
    i = lax.axis_index("exp")
    odd = lax.rem(r, 2)
    cl_own = r // 2

    def zdev(k):
        return lax.rem(r + k + Z, Z)

    w_copy = pltpu.make_async_copy(w3, W3V, loc.at[0])
    dn_copy = pltpu.make_async_copy(dn, DN, loc.at[1])
    own_copy = pltpu.make_async_copy(
        tok.at[:, pl.ds(pl.multiple_of(r * DS, 128), DS)],
        T.at[odd, pl.ds(pl.multiple_of(cl_own * TOK, TOK), TOK)],
        loc.at[2],
    )
    own_meta = pltpu.make_async_copy(meta, M.at[odd, cl_own], loc.at[3])
    own_copy.start()
    own_meta.start()
    w_copy.start()
    dn_copy.start()

    barrier = pltpu.get_barrier_semaphore()

    @pl.loop(1, Z)
    def _(k):
        pl.semaphore_signal(barrier, inc=1, device_id=(zdev(k), i), device_id_type=MESH)

    @pl.loop(1, E)
    def _(k):
        pl.semaphore_signal(barrier, inc=1, device_id=(r, lax.rem(i + k, E)), device_id_type=MESH)

    pl.semaphore_wait(barrier, Z - 1 + E - 1)

    def p1_pair(k):
        to = zdev(k)
        a = pltpu.make_async_remote_copy(
            src_ref=tok.at[:, pl.ds(pl.multiple_of(to * DS, 128), DS)],
            dst_ref=T.at[odd, pl.ds(pl.multiple_of(cl_own * TOK, TOK), TOK)],
            send_sem=p1s.at[k],
            recv_sem=p1r.at[odd, cl_own],
            device_id=(to, i),
            device_id_type=MESH,
        )
        b = pltpu.make_async_remote_copy(
            src_ref=meta,
            dst_ref=M.at[odd, cl_own],
            send_sem=m1s.at[k],
            recv_sem=m1r.at[odd, cl_own],
            device_id=(to, i),
            device_id_type=MESH,
        )
        return a, b

    def p1_send():
        @pl.loop(1, Z)
        def _(k):
            a, b = p1_pair(k)
            b.start()
            a.start()

    def p1_wait(h):
        for cl in range(4):
            @pl.when(r != 2 * cl + h)
            def _():
                pltpu.make_async_remote_copy(
                    src_ref=T.at[h, pl.ds(cl * TOK, TOK)],
                    dst_ref=T.at[h, pl.ds(cl * TOK, TOK)],
                    send_sem=p1s.at[0],
                    recv_sem=p1r.at[h, cl],
                    device_id=(zdev(1), i),
                    device_id_type=MESH,
                ).wait_recv()
                pltpu.make_async_remote_copy(
                    src_ref=meta,
                    dst_ref=M.at[h, cl],
                    send_sem=m1s.at[0],
                    recv_sem=m1r.at[h, cl],
                    device_id=(zdev(1), i),
                    device_id_type=MESH,
                ).wait_recv()

    def gather(h):
        rows = lax.broadcasted_iota(jnp.int32, (ROWS, 128), 0).astype(jnp.float32)
        for p in range(2):
            m = jnp.maximum(M[h, 2 * p], M[h, 2 * p + 1])
            hit0 = rows == m[0:1, :]
            hit1 = rows == m[1:2, :]
            DM[:, p * 128:(p + 1) * 128] = jnp.where(hit0 | hit1, 1.0, 0.0).astype(jnp.bfloat16)
            CT[h, :, p * 128:(p + 1) * 128] = (
                jnp.where(hit0, m[2:3, :], 0.0) + jnp.where(hit1, m[3:4, :], 0.0)
            ).astype(jnp.bfloat16)

        @pl.loop(0, 4)
        def _(q):
            at = pl.ds(pl.multiple_of(q * 128, 128), 128)
            G[h, at, :] = jnp.dot(DM[at, :], T[h], preferred_element_type=jnp.float32).astype(jnp.bfloat16)

    def plane_copy(src, dst, h, k, ssem, rsem):
        to = lax.rem(i + k, E)
        return pltpu.make_async_remote_copy(
            src_ref=src.at[h, pl.ds(pl.multiple_of(to * BLK, BLK), BLK)],
            dst_ref=dst.at[h, pl.ds(pl.multiple_of(i * BLK, BLK), BLK)],
            send_sem=ssem.at[h],
            recv_sem=rsem.at[h],
            device_id=(r, to),
            device_id_type=MESH,
        )

    def plane_send(src, dst, h, ssem, rsem):
        @pl.loop(1, E)
        def _(k):
            plane_copy(src, dst, h, k, ssem, rsem).start()

        own = pl.ds(pl.multiple_of(i * BLK, BLK), BLK)
        dst[h, own, :] = src[h, own, :]

    def plane_all(src, dst, h, ssem, rsem):
        most = pl.ds(0, ROWS - BLK)
        return pltpu.make_async_remote_copy(
            src_ref=src.at[h, most],
            dst_ref=dst.at[h, most],
            send_sem=ssem.at[h],
            recv_sem=rsem.at[h],
            device_id=(r, lax.rem(i + 1, E)),
            device_id_type=MESH,
        )

    def up(h):
        @pl.loop(0, 8)
        def _(n):
            at = pl.ds(pl.multiple_of(n * 256, 256), 256)
            PRE[h, :, at] = jnp.dot(X[h], W[:, at], preferred_element_type=jnp.float32)

    def rs_copy(h, way, sub, d):
        step = 1 if way == 0 else -1
        return pltpu.make_async_remote_copy(
            src_ref=RSS.at[h, way, sub, d - 1],
            dst_ref=RSR.at[h, way, sub, d - 1],
            send_sem=rss.at[h, way, sub, d - 1],
            recv_sem=rsr.at[h, way, sub, d - 1],
            device_id=(zdev(step), i),
            device_id_type=MESH,
        )

    def decode(h, way, sub, d):
        q = RSR[h, way, sub, d - 1]
        scale = jnp.exp2(q[:, 2 * FF:].astype(jnp.float32)) * (1.0 / LEVELS)
        return q, scale

    def rs_send(h, way, sub, d):
        owner = zdev(d if way == 0 else -d)
        at = pl.ds(pl.multiple_of(owner * CH + sub * SUB, SUB), SUB)
        far = FAR[h][way]
        s = PRE[h, at, :]
        if d < far:
            rs_copy(h, way, sub, d + 1).wait_recv()
            q, scale = decode(h, way, sub, d + 1)
            s = s + q[:, :2 * FF].astype(jnp.float32) * jnp.tile(scale, (1, 16))
        most = jnp.maximum(jnp.max(jnp.abs(s), axis=1, keepdims=True), 1e-30)
        expo = jnp.ceil(jnp.log2(most))
        code = jnp.round(s * (jnp.exp2(-expo) * LEVELS))
        RSS[h, way, sub, d - 1, :, :2 * FF] = code.astype(jnp.int32).astype(jnp.int16)
        RSS[h, way, sub, d - 1, :, 2 * FF:] = jnp.broadcast_to(expo, (SUB, 128)).astype(jnp.int32).astype(jnp.int16)
        rs_copy(h, way, sub, d).start()

    def ag_copy(h, way, sub, k):
        step = 1 if way == 0 else -1
        origin = zdev(-(k - 1) * step)
        at = pl.ds(pl.multiple_of(origin * CH + sub * SUB, SUB), SUB)
        return pltpu.make_async_remote_copy(
            src_ref=HD.at[h, at],
            dst_ref=HD.at[h, at],
            send_sem=ags.at[h, way, sub, k - 1],
            recv_sem=agr.at[h, way, sub, k - 1],
            device_id=(zdev(step), i),
            device_id_type=MESH,
        )

    def ag_wait(h, way, sub, k):
        step = 1 if way == 0 else -1
        origin = zdev(-k * step)
        at = pl.ds(pl.multiple_of(origin * CH + sub * SUB, SUB), SUB)
        pltpu.make_async_remote_copy(
            src_ref=HD.at[h, at],
            dst_ref=HD.at[h, at],
            send_sem=ags.at[h, way, sub, k - 1],
            recv_sem=agr.at[h, way, sub, k - 1],
            device_id=(zdev(step), i),
            device_id_type=MESH,
        ).wait_recv()

    def finish(h, sub):
        at = pl.ds(pl.multiple_of(r * CH + sub * SUB, SUB), SUB)
        s = PRE[h, at, :]
        for way in range(2):
            rs_copy(h, way, sub, 1).wait_recv()
            q, scale = decode(h, way, sub, 1)
            s = s + q[:, :2 * FF].astype(jnp.float32) * jnp.tile(scale, (1, 16))
        g = s[:, :FF]
        HD[h, at, :] = (g / (1.0 + jnp.exp(-g)) * s[:, FF:]).astype(jnp.bfloat16)
        for way in range(2):
            ag_copy(h, way, sub, 1).start()

    def ag_step(h, way, sub, k):
        ag_wait(h, way, sub, k)
        if k < FAR[h][way]:
            ag_copy(h, way, sub, k + 1).start()

    def down(h):
        @pl.loop(0, 7)
        def _(n):
            at = pl.ds(pl.multiple_of(n * 128, 128), 128)
            OUT[h, :, at] = jnp.dot(HD[h], DN[:, at], preferred_element_type=jnp.float32).astype(jnp.bfloat16)

    def combine(h):
        CB[h] = lax.dot_general(
            CT[h], B[h], (((0,), (0,)), ((), ())), preferred_element_type=jnp.float32
        ).astype(jnp.bfloat16)

    mine = pl.ds(pl.multiple_of(r * DS, 128), DS)

    def p10_copy(h, cl):
        return pltpu.make_async_remote_copy(
            src_ref=CB.at[h, pl.ds(cl * TOK, TOK)],
            dst_ref=comb_out.at[:, mine],
            send_sem=p10s.at[h, cl],
            recv_sem=p10r.at[r],
            device_id=(2 * cl + h, i),
            device_id_type=MESH,
        )

    def p10_self(h, cl):
        return pltpu.make_async_copy(CB.at[h, pl.ds(cl * TOK, TOK)], comb_out.at[:, mine], loc.at[4])

    def p10_send(h):
        for cl in range(4):
            @pl.when(r != 2 * cl + h)
            def _():
                p10_copy(h, cl).start()

            @pl.when(r == 2 * cl + h)
            def _():
                p10_self(h, cl).start()

    def hessian():
        at = pl.ds(pl.multiple_of(r * 128, 128), 128)
        total = lax.dot_general(
            HD[0, :, at], HD[0], (((0,), (0,)), ((), ())), preferred_element_type=jnp.float32
        ) + lax.dot_general(
            HD[1, :, at], HD[1], (((0,), (0,)), ((), ())), preferred_element_type=jnp.float32
        )
        hess_out[...] = total * (2.0 / 1024.0)

    @pl.when(odd == 0)
    def _():
        p1_send()

    w_copy.wait()

    @pl.loop(0, 14)
    def _(n):
        at = pl.ds(pl.multiple_of(n * 64, 64), 64)
        W[at, :FF] = W3V[at, 0, :]
        W[at, FF:] = W3V[at, 1, :]

    own_copy.wait()
    own_meta.wait()
    p1_wait(0)

    @pl.when(odd == 1)
    def _():
        p1_send()

    gather(0)
    plane_send(G, X, 0, p3s, p3r)
    p1_wait(1)
    gather(1)
    plane_send(G, X, 1, p3s, p3r)

    def rs_round(h, steps):
        for back in steps:
            for sub in range(NSUB):
                for way in range(2):
                    d = FAR[h][way] - back
                    if d >= 1:
                        rs_send(h, way, sub, d)

    plane_all(G, X, 0, p3s, p3r).wait_recv()
    up(0)
    rs_round(0, [0, 1])
    plane_all(G, X, 1, p3s, p3r).wait_recv()
    up(1)
    rs_round(0, [2])
    rs_round(1, [0])
    rs_round(0, [3])
    for sub in range(NSUB):
        finish(0, sub)
    rs_round(1, [1])
    for k in range(1, 5):
        for sub in range(NSUB):
            for way in range(2):
                if k <= FAR[0][way]:
                    ag_step(0, way, sub, k)
        if k == 1:
            rs_round(1, [2])
        if k == 3:
            rs_round(1, [3])
            for sub in range(NSUB):
                finish(1, sub)
    dn_copy.wait()
    down(0)
    plane_send(OUT, B, 0, p8s, p8r)
    for k in range(1, 5):
        for sub in range(NSUB):
            for way in range(2):
                if k <= FAR[1][way]:
                    ag_step(1, way, sub, k)
    down(1)
    plane_send(OUT, B, 1, p8s, p8r)
    hessian()
    for h in range(2):
        plane_all(OUT, B, h, p8s, p8r).wait_recv()
        combine(h)
        p10_send(h)

    @pl.loop(1, Z)
    def _(k):
        a, b = p1_pair(k)
        a.wait_send()
        b.wait_send()

    for h in range(2):
        plane_all(G, X, h, p3s, p3r).wait_send()
        plane_all(OUT, B, h, p8s, p8r).wait_send()
        for way in range(2):
            for sub in range(NSUB):
                for d in range(1, FAR[h][way] + 1):
                    rs_copy(h, way, sub, d).wait_send()
                    ag_copy(h, way, sub, d).wait_send()
        for cl in range(4):
            @pl.when(r != 2 * cl + h)
            def _():
                p10_copy(h, cl).wait_send()

            @pl.when(r == 2 * cl + h)
            def _():
                p10_self(h, cl).wait()

    @pl.loop(1, Z)
    def _(k):
        src = zdev(k)
        pltpu.make_async_remote_copy(
            src_ref=CB.at[0, pl.ds(0, TOK)],
            dst_ref=comb_out.at[:, pl.ds(pl.multiple_of(src * DS, 128), DS)],
            send_sem=p10s.at[0, 0],
            recv_sem=p10r.at[src],
            device_id=(zdev(1), i),
            device_id_type=MESH,
        ).wait_recv()


def local(tokens, expert_ids, combine_weights, gate_up_weight, down_weight):
    r = lax.axis_index("rep")
    flat = expert_ids.reshape(-1)
    onehot = (flat[:, None] == jnp.arange(E, dtype=jnp.int32)[None, :]).astype(jnp.int32)
    rank = jnp.sum((jnp.cumsum(onehot, axis=0) - onehot) * onehot, axis=1)
    pos = (flat * BLK + (r // 2) * SLOT + rank).reshape(TOK, 2).astype(jnp.float32).T
    wts = combine_weights.astype(jnp.float32).T
    both = jnp.concatenate([pos, wts, jnp.zeros((4, TOK), jnp.float32)], axis=0)
    fill = jnp.concatenate(
        [jnp.full((2, TOK), -1.0, jnp.float32), jnp.zeros((6, TOK), jnp.float32)], axis=0
    )
    meta = jnp.where(
        lax.rem(r // 2, 2) == 0,
        jnp.concatenate([both, fill], axis=1),
        jnp.concatenate([fill, both], axis=1),
    )
    bf, f32 = jnp.bfloat16, jnp.float32
    dma = pltpu.SemaphoreType.DMA
    comb, hess = pl.pallas_call(
        kernel,
        out_shape=(
            jax.ShapeDtypeStruct((TOK, D), bf),
            jax.ShapeDtypeStruct((128, FF), f32),
        ),
        in_specs=[
            pl.BlockSpec(memory_space=pl.ANY),
            pl.BlockSpec(memory_space=pltpu.VMEM),
            pl.BlockSpec(memory_space=pl.ANY),
            pl.BlockSpec(memory_space=pl.ANY),
        ],
        out_specs=(
            pl.BlockSpec(memory_space=pl.ANY),
            pl.BlockSpec(memory_space=pltpu.VMEM),
        ),
        scratch_shapes=[
            pltpu.VMEM((2, 4 * TOK, DS), bf),
            pltpu.VMEM((2, 4, 8, 128), f32),
            pltpu.VMEM((ROWS, 4 * TOK), bf),
            pltpu.VMEM((2, ROWS, 4 * TOK), bf),
            pltpu.VMEM((2, ROWS, DS), bf),
            pltpu.VMEM((2, ROWS, DS), bf),
            pltpu.VMEM((DS, 2, FF), bf),
            pltpu.VMEM((DS, 2 * FF), bf),
            pltpu.VMEM((FF, DS), bf),
            pltpu.VMEM((2, ROWS, 2 * FF), f32),
            pltpu.VMEM((2, 2, NSUB, 4, SUB, MSG), jnp.int16),
            pltpu.VMEM((2, 2, NSUB, 4, SUB, MSG), jnp.int16),
            pltpu.VMEM((2, ROWS, FF), bf),
            pltpu.VMEM((2, ROWS, DS), bf),
            pltpu.VMEM((2, ROWS, DS), bf),
            pltpu.VMEM((2, 4 * TOK, DS), bf),
            dma((5,)),
            dma((Z,)),
            dma((2, 4)),
            dma((Z,)),
            dma((2, 4)),
            dma((2,)),
            dma((2,)),
            dma((2, 2, NSUB, 4)),
            dma((2, 2, NSUB, 4)),
            dma((2, 2, NSUB, 4)),
            dma((2, 2, NSUB, 4)),
            dma((2,)),
            dma((2,)),
            dma((2, 4)),
            dma((Z,)),
        ],
        compiler_params=pltpu.CompilerParams(
            collective_id=0, has_side_effects=True, vmem_limit_bytes=60 * 1024 * 1024
        ),
        name="moe",
    )(tokens, meta, gate_up_weight[0], down_weight[0])
    return comb.astype(jnp.float32), hess[None]


def solution(mesh):
    return jax.shard_map(
        local,
        mesh=mesh,
        in_specs=(
            P(("rep", "exp"), None),
            P(("rep", "exp"), None),
            P(("rep", "exp"), None),
            P("exp", "rep", None, None),
            P("exp", None, "rep"),
        ),
        out_specs=(P(("rep", "exp"), None), P("exp", "rep", None)),
        check_vma=False,
    )
```

```python
import functools

import jax
import jax.numpy as jnp
from jax import lax
from jax.experimental import pallas as pl
from jax.experimental.pallas import tpu as pltpu
from jax.sharding import PartitionSpec as P

MESH = pl.DeviceIdType.MESH
Z = 8
E = 32
TOK = 64
SLOT = 4
D = 7168
DS = D // Z
FF = 1024
ROWS = 512
HALF = 16
BLK = 32
CH = ROWS // Z
NSUB = 2
SUB = CH // NSUB
MSG = 2 * FF + 128
LEVELS = 32000.0
FAR = ((4, 3), (3, 4))
PARTS = ((0, 512), (512, 384))


def kernel(
    tok, ids, wts, w3, dn, comb_out, hess_out,
    META, T, M, DM, CT, G, X, W3V, W, DN, PRE, RSS, RSR, HD, OUT, B, CB,
    go, loc, p1s, p1r, m1s, m1r, p3s, p3r, rss, rsr, ags, agr, p8s, p8r, p10s, p10r,
):
    r = lax.axis_index("rep")
    i = lax.axis_index("exp")
    core = lax.rem(i, 2)
    pair = i // 2
    zh_own, cl_own = r // 4, lax.rem(r, 4)

    def zdev(k):
        return lax.rem(r + k + Z, Z)

    w_copy = pltpu.make_async_copy(w3, W3V, loc.at[0])
    dn_copy = pltpu.make_async_copy(dn, DN, loc.at[1])
    own_copy = pltpu.make_async_copy(
        tok.at[:, pl.ds(pl.multiple_of(r * DS, 128), DS)],
        T.at[zh_own, pl.ds(pl.multiple_of(cl_own * TOK, TOK), TOK)],
        loc.at[2],
    )
    own_copy.start()
    w_copy.start()
    dn_copy.start()

    barrier = pltpu.get_barrier_semaphore()

    @pl.loop(1, Z)
    def _(k):
        pl.semaphore_signal(barrier, inc=1, device_id=(zdev(k), i), device_id_type=MESH)

    @pl.loop(1, E)
    def _(k):
        pl.semaphore_signal(barrier, inc=1, device_id=(r, lax.rem(i + k, E)), device_id_type=MESH)

    pl.semaphore_wait(barrier, Z - 1 + E - 1)

    def tok_copy(k, part):
        to = zdev(k)
        lo, n = PARTS[part]
        return pltpu.make_async_remote_copy(
            src_ref=tok.at[:, pl.ds(pl.multiple_of(to * DS + lo, 128), n)],
            dst_ref=T.at[zh_own, pl.ds(pl.multiple_of(cl_own * TOK, TOK), TOK), pl.ds(lo, n)],
            send_sem=p1s.at[k, part],
            recv_sem=p1r.at[r, part],
            device_id=(to, i),
            device_id_type=MESH,
        )

    def meta_copy(k):
        return pltpu.make_async_remote_copy(
            src_ref=META,
            dst_ref=M.at[zh_own, cl_own],
            send_sem=m1s.at[k],
            recv_sem=m1r.at[r],
            device_id=(zdev(k), i),
            device_id_type=MESH,
        )

    def p1_send():
        for part in range(2):
            @pl.loop(1, Z)
            def _(k):
                tok_copy(k, part).start()

    def meta_send():
        row = ids[...].astype(jnp.float32)
        row = jnp.concatenate([row[0:1, :], row[1:2, :]], axis=1)
        hot = lax.broadcasted_iota(jnp.int32, (E, 2 * TOK), 0).astype(jnp.float32) == row
        hot = jnp.where(hot, 1.0, 0.0)
        earlier = lax.broadcasted_iota(jnp.int32, (2 * TOK, 2 * TOK), 0) < lax.broadcasted_iota(
            jnp.int32, (2 * TOK, 2 * TOK), 1
        )
        count = jnp.dot(
            hot.astype(jnp.bfloat16),
            jnp.where(earlier, 1.0, 0.0).astype(jnp.bfloat16),
            preferred_element_type=jnp.float32,
        )
        rank = jnp.sum(hot * count, axis=0, keepdims=True)
        pos = row * HALF + rank + (cl_own * SLOT).astype(jnp.float32)
        w = wts[...].astype(jnp.float32)
        four = jnp.concatenate([pos[:, :TOK], pos[:, TOK:], w], axis=0)
        fill = jnp.where(lax.broadcasted_iota(jnp.int32, (4, TOK), 0) < 2, -1.0, 0.0)
        wide = jnp.where(
            lax.rem(cl_own, 2) == 0,
            jnp.concatenate([four, fill], axis=1),
            jnp.concatenate([fill, four], axis=1),
        )
        META[...] = jnp.concatenate([wide, wide], axis=0)
        M[zh_own, cl_own] = jnp.concatenate([wide, wide], axis=0)

        @pl.loop(1, Z)
        def _(k):
            meta_copy(k).start()

    def meta_wait():
        @pl.loop(1, Z)
        def _(k):
            c = zdev(k)
            pltpu.make_async_remote_copy(
                src_ref=META,
                dst_ref=M.at[c // 4, lax.rem(c, 4)],
                send_sem=m1s.at[k],
                recv_sem=m1r.at[c],
                device_id=(c, i),
                device_id_type=MESH,
            ).wait_recv()

    def p1_wait(part):
        lo, n = PARTS[part]

        @pl.loop(1, Z)
        def _(k):
            c = zdev(k)
            at = pl.ds(pl.multiple_of(lax.rem(c, 4) * TOK, TOK), TOK)
            pltpu.make_async_remote_copy(
                src_ref=T.at[c // 4, at, pl.ds(lo, n)],
                dst_ref=T.at[c // 4, at, pl.ds(lo, n)],
                send_sem=p1s.at[k, part],
                recv_sem=p1r.at[c, part],
                device_id=(c, i),
                device_id_type=MESH,
            ).wait_recv()

    def routes():
        rows = lax.broadcasted_iota(jnp.int32, (ROWS, 128), 0).astype(jnp.float32)
        for zh in range(2):
            for p in range(2):
                m = jnp.maximum(M[zh, 2 * p], M[zh, 2 * p + 1])
                hit0 = rows == m[0:1, :]
                hit1 = rows == m[1:2, :]
                DM[zh, :, p * 128:(p + 1) * 128] = jnp.where(hit0 | hit1, 1.0, 0.0).astype(jnp.bfloat16)
                CT[zh, :, p * 128:(p + 1) * 128] = (
                    jnp.where(hit0, m[2:3, :], 0.0) + jnp.where(hit1, m[3:4, :], 0.0)
                ).astype(jnp.bfloat16)

    def gather(part):
        lo, n = PARTS[part]
        for zh in range(2):
            @pl.loop(0, 4)
            def _(q):
                at = pl.ds(pl.multiple_of(q * 128, 128), 128)
                got = jnp.dot(DM[zh, at, :], T[zh, :, lo:lo + n], preferred_element_type=jnp.float32)
                G[pl.ds(q * 8, 8), zh * HALF:(zh + 1) * HALF, lo:lo + n] = got.astype(jnp.bfloat16).reshape(8, HALF, n)

    def p3_copy(part, k):
        to = lax.rem(i + k, E)
        lo, n = PARTS[part]
        return pltpu.make_async_remote_copy(
            src_ref=G.at[to, :, pl.ds(lo, n)],
            dst_ref=X.at[core, pl.ds(pl.multiple_of(pair * BLK, BLK), BLK), pl.ds(lo, n)],
            send_sem=p3s.at[part],
            recv_sem=p3r.at[core, part],
            device_id=(r, to),
            device_id_type=MESH,
        )

    def p3_send(part):
        @pl.loop(1, E)
        def _(k):
            p3_copy(part, k).start()

        lo, n = PARTS[part]
        X[core, pl.ds(pl.multiple_of(pair * BLK, BLK), BLK), lo:lo + n] = G[i, :, lo:lo + n]

    def p3_sent(part):
        lo, n = PARTS[part]
        return pltpu.make_async_remote_copy(
            src_ref=G.at[pl.ds(0, E - 1), :, pl.ds(lo, n)],
            dst_ref=G.at[pl.ds(0, E - 1), :, pl.ds(lo, n)],
            send_sem=p3s.at[part],
            recv_sem=p3r.at[0, part],
            device_id=(r, lax.rem(i + 1, E)),
            device_id_type=MESH,
        )

    def p3_rows(h, part, rows):
        lo, n = PARTS[part]
        return pltpu.make_async_remote_copy(
            src_ref=X.at[h, pl.ds(0, rows), pl.ds(lo, n)],
            dst_ref=X.at[h, pl.ds(0, rows), pl.ds(lo, n)],
            send_sem=p3s.at[part],
            recv_sem=p3r.at[h, part],
            device_id=(r, lax.rem(i + 1, E)),
            device_id_type=MESH,
        )

    def p3_wait(h):
        for part in range(2):
            @pl.when(core == h)
            def _():
                p3_rows(h, part, ROWS - BLK).wait_recv()

            @pl.when(core != h)
            def _():
                p3_rows(h, part, ROWS).wait_recv()

    def p8_copy(h, p):
        return pltpu.make_async_remote_copy(
            src_ref=OUT.at[h, pl.ds(pl.multiple_of(p * BLK, BLK), BLK)],
            dst_ref=B.at[i],
            send_sem=p8s.at[h],
            recv_sem=p8r,
            device_id=(r, 2 * p + h),
            device_id_type=MESH,
        )

    def p8_wait():
        pltpu.make_async_remote_copy(
            src_ref=B.at[pl.ds(0, E - 1)],
            dst_ref=B.at[pl.ds(0, E - 1)],
            send_sem=p8s.at[0],
            recv_sem=p8r,
            device_id=(r, lax.rem(i + 1, E)),
            device_id_type=MESH,
        ).wait_recv()

    def p8_sent(h, rows):
        return pltpu.make_async_remote_copy(
            src_ref=OUT.at[h, pl.ds(0, rows)],
            dst_ref=OUT.at[h, pl.ds(0, rows)],
            send_sem=p8s.at[h],
            recv_sem=p8r,
            device_id=(r, lax.rem(i + 1, E)),
            device_id_type=MESH,
        )

    def group(owner):
        return lax.rem(owner + i, Z)

    def chunk(owner):
        return pl.ds(pl.multiple_of(group(owner) * CH, CH), CH)

    def piece(owner, sub):
        return pl.ds(pl.multiple_of(group(owner) * CH + sub * SUB, SUB), SUB)

    def up(h, owner):
        at = chunk(owner)

        @pl.loop(0, 4)
        def _(n):
            cols = pl.ds(pl.multiple_of(n * 512, 512), 512)
            PRE[h, at, cols] = jnp.dot(X[h, at, :], W[:, cols], preferred_element_type=jnp.float32)

    def up_part(h, q):
        @pl.loop(2 * q, 2 * q + 2)
        def _(n):
            cols = pl.ds(pl.multiple_of(n * 256, 256), 256)
            PRE[h, :, cols] = jnp.dot(X[h], W[:, cols], preferred_element_type=jnp.float32)

    def down(h, owner):
        at = chunk(owner)
        OUT[h, at, :] = jnp.dot(HD[h, at, :], DN[...], preferred_element_type=jnp.float32).astype(jnp.bfloat16)
        for j in range(CH // BLK):
            p = group(owner) * (CH // BLK) + j
            to = 2 * p + h

            @pl.when(to != i)
            def _():
                p8_copy(h, p).start()

            @pl.when(to == i)
            def _():
                B[i] = OUT[h, pl.ds(pl.multiple_of(pair * BLK, BLK), BLK), :]

    def rs_copy(h, way, sub, d):
        step = 1 if way == 0 else -1
        return pltpu.make_async_remote_copy(
            src_ref=RSS.at[h, way, sub, d - 1],
            dst_ref=RSR.at[h, way, sub, d - 1],
            send_sem=rss.at[h, way, sub, d - 1],
            recv_sem=rsr.at[h, way, sub, d - 1],
            device_id=(zdev(step), i),
            device_id_type=MESH,
        )

    def decode(h, way, sub, d):
        q = RSR[h, way, sub, d - 1]
        scale = jnp.exp2(q[:, 2 * FF:].astype(jnp.float32)) * (1.0 / LEVELS)
        return q, scale

    def rs_send(h, way, sub, d):
        owner = zdev(d if way == 0 else -d)
        far = FAR[h][way]
        s = PRE[h, piece(owner, sub), :]
        if d < far:
            rs_copy(h, way, sub, d + 1).wait_recv()
            q, scale = decode(h, way, sub, d + 1)
            s = s + q[:, :2 * FF].astype(jnp.float32) * jnp.tile(scale, (1, 16))
        most = jnp.maximum(jnp.max(jnp.abs(s), axis=1, keepdims=True), 1e-30)
        expo = jnp.ceil(jnp.log2(most))
        code = jnp.round(s * (jnp.exp2(-expo) * LEVELS))
        RSS[h, way, sub, d - 1, :, :2 * FF] = code.astype(jnp.int32).astype(jnp.int16)
        RSS[h, way, sub, d - 1, :, 2 * FF:] = jnp.broadcast_to(expo, (SUB, 128)).astype(jnp.int32).astype(jnp.int16)
        rs_copy(h, way, sub, d).start()

    def ag_copy(h, way, sub, k):
        step = 1 if way == 0 else -1
        origin = zdev(-(k - 1) * step)
        at = piece(origin, sub)
        return pltpu.make_async_remote_copy(
            src_ref=HD.at[h, at],
            dst_ref=HD.at[h, at],
            send_sem=ags.at[h, way, sub, k - 1],
            recv_sem=agr.at[h, way, sub, k - 1],
            device_id=(zdev(step), i),
            device_id_type=MESH,
        )

    def ag_wait(h, way, sub, k):
        step = 1 if way == 0 else -1
        origin = zdev(-k * step)
        at = piece(origin, sub)
        pltpu.make_async_remote_copy(
            src_ref=HD.at[h, at],
            dst_ref=HD.at[h, at],
            send_sem=ags.at[h, way, sub, k - 1],
            recv_sem=agr.at[h, way, sub, k - 1],
            device_id=(zdev(step), i),
            device_id_type=MESH,
        ).wait_recv()

    def finish(h, sub):
        at = piece(r, sub)
        s = PRE[h, at, :]
        for way in range(2):
            rs_copy(h, way, sub, 1).wait_recv()
            q, scale = decode(h, way, sub, 1)
            s = s + q[:, :2 * FF].astype(jnp.float32) * jnp.tile(scale, (1, 16))
        g = s[:, :FF]
        HD[h, at, :] = (g / (1.0 + jnp.exp(-g)) * s[:, FF:]).astype(jnp.bfloat16)
        for way in range(2):
            ag_copy(h, way, sub, 1).start()

    def ag_step(h, way, sub, k):
        ag_wait(h, way, sub, k)
        if k < FAR[h][way]:
            ag_copy(h, way, sub, k + 1).start()

    def combine():
        for zh in range(2):
            back = B[:, zh * HALF:(zh + 1) * HALF, :].reshape(ROWS, DS)
            CB[zh * 4 * TOK:(zh + 1) * 4 * TOK, :] = lax.dot_general(
                CT[zh], back, (((0,), (0,)), ((), ())), preferred_element_type=jnp.float32
            ).astype(jnp.bfloat16)

    mine = pl.ds(pl.multiple_of(r * DS, 128), DS)

    def p10_copy(k):
        c = zdev(k)
        return pltpu.make_async_remote_copy(
            src_ref=CB.at[pl.ds(pl.multiple_of(c * TOK, TOK), TOK)],
            dst_ref=comb_out.at[:, mine],
            send_sem=p10s.at[c],
            recv_sem=p10r.at[r],
            device_id=(c, i),
            device_id_type=MESH,
        )

    def p10_self():
        return pltpu.make_async_copy(
            CB.at[pl.ds(pl.multiple_of(r * TOK, TOK), TOK)], comb_out.at[:, mine], loc.at[3]
        )

    def p10_send(h, ks):
        @pl.when(core == h)
        def _():
            for k in ks:
                p10_copy(k).start()

    def hessian():
        at = pl.ds(pl.multiple_of(r * 128, 128), 128)
        total = lax.dot_general(
            HD[0, :, at], HD[0], (((0,), (0,)), ((), ())), preferred_element_type=jnp.float32
        ) + lax.dot_general(
            HD[1, :, at], HD[1], (((0,), (0,)), ((), ())), preferred_element_type=jnp.float32
        )
        hess_out[...] = total * (2.0 / 1024.0)

    def layout(first, last):
        @pl.loop(first, last)
        def _(n):
            at = pl.ds(pl.multiple_of(n * 64, 64), 64)
            W[at, :FF] = W3V[at, 0, :]
            W[at, FF:] = W3V[at, 1, :]

    def ag(h, k, sub):
        for way in range(2):
            if k <= FAR[h][way]:
                ag_step(h, way, sub, k)

    def downs(h, k):
        for way in range(2):
            if k <= FAR[h][way]:
                down(h, zdev(-k if way == 0 else k))

    def hand_in(part, h):
        @pl.when(core == h)
        def _():
            p1_wait(part)
            gather(part)
            p3_send(part)

    def hand_out(h):
        @pl.when(core == h)
        def _():
            p8_wait()
            combine()
            p10_self().start()

    meta_send()

    @pl.when(core == 0)
    def _():
        p1_send()

    w_copy.wait()
    layout(0, 14)
    own_copy.wait()
    meta_wait()
    routes()
    hand_in(0, 0)
    hand_in(1, 0)

    @pl.when(core == 0)
    def _():
        pl.semaphore_signal(go, inc=1, device_id=(r, i + 1), device_id_type=MESH)

    @pl.when(core == 1)
    def _():
        pl.semaphore_wait(go, 1)
        p1_send()

    p3_wait(0)
    up(0, zdev(4))
    for sub in range(NSUB):
        rs_send(0, 0, sub, 4)
    up(0, zdev(-3))
    for sub in range(NSUB):
        rs_send(0, 1, sub, 3)
    for q in range(4):
        up_part(0, q)
    hand_in(0, 1)
    for sub in range(NSUB):
        rs_send(0, 0, sub, 3)
        rs_send(0, 1, sub, 2)
    hand_in(1, 1)
    for sub in range(NSUB):
        rs_send(0, 0, sub, 2)
        rs_send(0, 1, sub, 1)
    dn_copy.wait()
    p3_wait(1)
    up(1, zdev(-4))
    for sub in range(NSUB):
        rs_send(1, 1, sub, 4)
        rs_send(0, 0, sub, 1)
    for q in range(4):
        up_part(1, q)
    for sub in range(NSUB):
        finish(0, sub)
        rs_send(1, 0, sub, 3)
        rs_send(1, 1, sub, 3)
    down(0, r)
    for sub in range(NSUB):
        ag(0, 1, sub)
        rs_send(1, 0, sub, 2)
        rs_send(1, 1, sub, 2)
    downs(0, 1)
    for sub in range(NSUB):
        ag(0, 2, sub)
        rs_send(1, 0, sub, 1)
        rs_send(1, 1, sub, 1)
    downs(0, 2)
    for sub in range(NSUB):
        ag(0, 3, sub)
        finish(1, sub)
    for sub in range(NSUB):
        ag(0, 4, sub)
    downs(0, 3)
    downs(0, 4)
    down(1, r)
    for sub in range(NSUB):
        ag(1, 1, sub)
    downs(1, 1)
    hand_out(0)
    p10_send(0, (4, 1))
    for sub in range(NSUB):
        ag(1, 2, sub)
    p10_send(0, (3, 7))
    downs(1, 2)
    for sub in range(NSUB):
        ag(1, 3, sub)
    p10_send(0, (5, 2))
    downs(1, 3)
    for sub in range(NSUB):
        ag(1, 4, sub)
    p10_send(0, (6,))
    downs(1, 4)
    hessian()
    hand_out(1)
    p10_send(1, (4, 3, 5, 2, 6, 1, 7))

    @pl.loop(1, Z)
    def _(k):
        for part in range(2):
            tok_copy(k, part).wait_send()
        meta_copy(k).wait_send()
        p10_copy(k).wait_send()

    p10_self().wait()
    for part in range(2):
        p3_sent(part).wait_send()

    for h in range(2):
        @pl.when(core == h)
        def _():
            p8_sent(h, ROWS - BLK).wait_send()

        @pl.when(core != h)
        def _():
            p8_sent(h, ROWS).wait_send()

        for way in range(2):
            for sub in range(NSUB):
                for d in range(1, FAR[h][way] + 1):
                    rs_copy(h, way, sub, d).wait_send()
                    ag_copy(h, way, sub, d).wait_send()

    @pl.loop(1, Z)
    def _(k):
        src = zdev(k)
        pltpu.make_async_remote_copy(
            src_ref=CB.at[pl.ds(0, TOK)],
            dst_ref=comb_out.at[:, pl.ds(pl.multiple_of(src * DS, 128), DS)],
            send_sem=p10s.at[src],
            recv_sem=p10r.at[src],
            device_id=(src, i),
            device_id_type=MESH,
        ).wait_recv()


def local(tokens, expert_ids, combine_weights, gate_up_weight, down_weight):
    bf, f32 = jnp.bfloat16, jnp.float32
    dma = pltpu.SemaphoreType.DMA
    comb, hess = pl.pallas_call(
        kernel,
        out_shape=(
            jax.ShapeDtypeStruct((TOK, D), bf),
            jax.ShapeDtypeStruct((128, FF), f32),
        ),
        in_specs=[
            pl.BlockSpec(memory_space=pl.ANY),
            pl.BlockSpec(memory_space=pltpu.VMEM),
            pl.BlockSpec(memory_space=pltpu.VMEM),
            pl.BlockSpec(memory_space=pl.ANY),
            pl.BlockSpec(memory_space=pl.ANY),
        ],
        out_specs=(
            pl.BlockSpec(memory_space=pl.ANY),
            pl.BlockSpec(memory_space=pltpu.VMEM),
        ),
        scratch_shapes=[
            pltpu.VMEM((8, 128), f32),
            pltpu.VMEM((2, 4 * TOK, DS), bf),
            pltpu.VMEM((2, 4, 8, 128), f32),
            pltpu.VMEM((2, ROWS, 4 * TOK), bf),
            pltpu.VMEM((2, ROWS, 4 * TOK), bf),
            pltpu.VMEM((E, BLK, DS), bf),
            pltpu.VMEM((2, ROWS, DS), bf),
            pltpu.VMEM((DS, 2, FF), bf),
            pltpu.VMEM((DS, 2 * FF), bf),
            pltpu.VMEM((FF, DS), bf),
            pltpu.VMEM((2, ROWS, 2 * FF), f32),
            pltpu.VMEM((2, 2, NSUB, 4, SUB, MSG), jnp.int16),
            pltpu.VMEM((2, 2, NSUB, 4, SUB, MSG), jnp.int16),
            pltpu.VMEM((2, ROWS, FF), bf),
            pltpu.VMEM((2, ROWS, DS), bf),
            pltpu.VMEM((E, BLK, DS), bf),
            pltpu.VMEM((Z * TOK, DS), bf),
            pltpu.SemaphoreType.REGULAR,
            dma((4,)),
            dma((Z, 2)),
            dma((Z, 2)),
            dma((Z,)),
            dma((Z,)),
            dma((2,)),
            dma((2, 2)),
            dma((2, 2, NSUB, 4)),
            dma((2, 2, NSUB, 4)),
            dma((2, 2, NSUB, 4)),
            dma((2, 2, NSUB, 4)),
            dma((2,)),
            dma,
            dma((Z,)),
            dma((Z,)),
        ],
        compiler_params=pltpu.CompilerParams(
            collective_id=0, has_side_effects=True, vmem_limit_bytes=60 * 1024 * 1024
        ),
        name="moe",
    )(tokens, expert_ids.T, combine_weights.T, gate_up_weight[0], down_weight[0])
    return comb.astype(jnp.float32), hess[None]


def solution(mesh):
    return jax.shard_map(
        local,
        mesh=mesh,
        in_specs=(
            P(("rep", "exp"), None),
            P(("rep", "exp"), None),
            P(("rep", "exp"), None),
            P("exp", "rep", None, None),
            P("exp", None, "rep"),
        ),
        out_specs=(P(("rep", "exp"), None), P("exp", "rep", None)),
        check_vma=False,
    )
```

```python
import functools

import jax
import jax.numpy as jnp
from jax import lax
from jax.experimental import pallas as pl
from jax.experimental.pallas import tpu as pltpu
from jax.sharding import PartitionSpec as P

MESH = pl.DeviceIdType.MESH
Z = 8
E = 32
TOK = 64
SLOT = 4
D = 7168
DS = D // Z
FF = 1024
ROWS = 512
HALF = 16
BLK = 32
CH = ROWS // Z
NSUB = 2
SUB = CH // NSUB
MSG = 2 * FF + 128
LEVELS = 32000.0
FAR = ((4, 3), (3, 4))
PARTS = ((0, 256), (256, 256), (512, 256), (768, 128))
NP = len(PARTS)
PIECES = [(k, part) for k in (4, 3, 5, 2, 6, 1, 7) for part in range(NP)]


def kernel(
    tok, ids, wts, w3, dn, comb_out, hess_out,
    META, T, M, DM, CT, G, X, W3V, W, DN, PRE, RSS, RSR, HD, OUT, B, CB,
    go, loc, p1s, p1r, m1s, m1r, p3s, p3r, rss, rsr, ags, agr, p8s, p8r, p10s, p10r,
):
    r = lax.axis_index("rep")
    i = lax.axis_index("exp")
    core = lax.rem(i, 2)
    pair = i // 2
    zh_own, cl_own = r // 4, lax.rem(r, 4)

    def zdev(k):
        return lax.rem(r + k + Z, Z)

    w_copy = pltpu.make_async_copy(w3, W3V, loc.at[0])
    dn_copy = pltpu.make_async_copy(dn, DN, loc.at[1])
    own_copy = pltpu.make_async_copy(
        tok.at[:, pl.ds(pl.multiple_of(r * DS, 128), DS)],
        T.at[zh_own, pl.ds(pl.multiple_of(cl_own * TOK, TOK), TOK)],
        loc.at[2],
    )
    own_copy.start()
    w_copy.start()
    dn_copy.start()

    barrier = pltpu.get_barrier_semaphore()

    @pl.loop(1, Z)
    def _(k):
        pl.semaphore_signal(barrier, inc=1, device_id=(zdev(k), i), device_id_type=MESH)

    @pl.loop(1, E)
    def _(k):
        pl.semaphore_signal(barrier, inc=1, device_id=(r, lax.rem(i + k, E)), device_id_type=MESH)

    pl.semaphore_wait(barrier, Z - 1 + E - 1)

    def tok_copy(k, part):
        to = zdev(k)
        lo, n = PARTS[part]
        return pltpu.make_async_remote_copy(
            src_ref=tok.at[:, pl.ds(pl.multiple_of(to * DS + lo, 128), n)],
            dst_ref=T.at[zh_own, pl.ds(pl.multiple_of(cl_own * TOK, TOK), TOK), pl.ds(lo, n)],
            send_sem=p1s.at[k, part],
            recv_sem=p1r.at[r, part],
            device_id=(to, i),
            device_id_type=MESH,
        )

    def meta_copy(k):
        return pltpu.make_async_remote_copy(
            src_ref=META,
            dst_ref=M.at[zh_own, cl_own],
            send_sem=m1s.at[k],
            recv_sem=m1r.at[r],
            device_id=(zdev(k), i),
            device_id_type=MESH,
        )

    def p1_send():
        for part in range(NP):
            @pl.loop(1, Z)
            def _(k):
                tok_copy(k, part).start()

    def meta_send():
        row = ids[...].astype(jnp.float32)
        row = jnp.concatenate([row[0:1, :], row[1:2, :]], axis=1)
        hot = lax.broadcasted_iota(jnp.int32, (E, 2 * TOK), 0).astype(jnp.float32) == row
        hot = jnp.where(hot, 1.0, 0.0)
        earlier = lax.broadcasted_iota(jnp.int32, (2 * TOK, 2 * TOK), 0) < lax.broadcasted_iota(
            jnp.int32, (2 * TOK, 2 * TOK), 1
        )
        count = jnp.dot(
            hot.astype(jnp.bfloat16),
            jnp.where(earlier, 1.0, 0.0).astype(jnp.bfloat16),
            preferred_element_type=jnp.float32,
        )
        rank = jnp.sum(hot * count, axis=0, keepdims=True)
        pos = row * HALF + rank + (cl_own * SLOT).astype(jnp.float32)
        w = wts[...].astype(jnp.float32)
        four = jnp.concatenate([pos[:, :TOK], pos[:, TOK:], w], axis=0)
        fill = jnp.where(lax.broadcasted_iota(jnp.int32, (4, TOK), 0) < 2, -1.0, 0.0)
        wide = jnp.where(
            lax.rem(cl_own, 2) == 0,
            jnp.concatenate([four, fill], axis=1),
            jnp.concatenate([fill, four], axis=1),
        )
        META[...] = jnp.concatenate([wide, wide], axis=0)
        M[zh_own, cl_own] = jnp.concatenate([wide, wide], axis=0)

        @pl.loop(1, Z)
        def _(k):
            meta_copy(k).start()

    def meta_wait():
        @pl.loop(1, Z)
        def _(k):
            c = zdev(k)
            pltpu.make_async_remote_copy(
                src_ref=META,
                dst_ref=M.at[c // 4, lax.rem(c, 4)],
                send_sem=m1s.at[k],
                recv_sem=m1r.at[c],
                device_id=(c, i),
                device_id_type=MESH,
            ).wait_recv()

    def p1_wait(part):
        lo, n = PARTS[part]

        @pl.loop(1, Z)
        def _(k):
            c = zdev(k)
            at = pl.ds(pl.multiple_of(lax.rem(c, 4) * TOK, TOK), TOK)
            pltpu.make_async_remote_copy(
                src_ref=T.at[c // 4, at, pl.ds(lo, n)],
                dst_ref=T.at[c // 4, at, pl.ds(lo, n)],
                send_sem=p1s.at[k, part],
                recv_sem=p1r.at[c, part],
                device_id=(c, i),
                device_id_type=MESH,
            ).wait_recv()

    def routes():
        rows = lax.broadcasted_iota(jnp.int32, (ROWS, 128), 0).astype(jnp.float32)
        for zh in range(2):
            for p in range(2):
                m = jnp.maximum(M[zh, 2 * p], M[zh, 2 * p + 1])
                hit0 = rows == m[0:1, :]
                hit1 = rows == m[1:2, :]
                DM[zh, :, p * 128:(p + 1) * 128] = jnp.where(hit0 | hit1, 1.0, 0.0).astype(jnp.bfloat16)
                CT[zh, :, p * 128:(p + 1) * 128] = (
                    jnp.where(hit0, m[2:3, :], 0.0) + jnp.where(hit1, m[3:4, :], 0.0)
                ).astype(jnp.bfloat16)

    def gather(part):
        lo, n = PARTS[part]
        for zh in range(2):
            @pl.loop(0, 4)
            def _(q):
                at = pl.ds(pl.multiple_of(q * 128, 128), 128)
                got = jnp.dot(DM[zh, at, :], T[zh, :, lo:lo + n], preferred_element_type=jnp.float32)
                G[pl.ds(q * 8, 8), zh * HALF:(zh + 1) * HALF, lo:lo + n] = got.astype(jnp.bfloat16).reshape(8, HALF, n)

    def p3_copy(part, k):
        to = lax.rem(i + k, E)
        lo, n = PARTS[part]
        return pltpu.make_async_remote_copy(
            src_ref=G.at[to, :, pl.ds(lo, n)],
            dst_ref=X.at[core, pl.ds(pl.multiple_of(pair * BLK, BLK), BLK), pl.ds(lo, n)],
            send_sem=p3s.at[part],
            recv_sem=p3r.at[core, part],
            device_id=(r, to),
            device_id_type=MESH,
        )

    def p3_send(part):
        @pl.loop(1, E)
        def _(k):
            p3_copy(part, k).start()

        lo, n = PARTS[part]
        X[core, pl.ds(pl.multiple_of(pair * BLK, BLK), BLK), lo:lo + n] = G[i, :, lo:lo + n]

    def p3_sent(part):
        lo, n = PARTS[part]
        return pltpu.make_async_remote_copy(
            src_ref=G.at[pl.ds(0, E - 1), :, pl.ds(lo, n)],
            dst_ref=G.at[pl.ds(0, E - 1), :, pl.ds(lo, n)],
            send_sem=p3s.at[part],
            recv_sem=p3r.at[0, part],
            device_id=(r, lax.rem(i + 1, E)),
            device_id_type=MESH,
        )

    def p3_rows(h, part, rows):
        lo, n = PARTS[part]
        return pltpu.make_async_remote_copy(
            src_ref=X.at[h, pl.ds(0, rows), pl.ds(lo, n)],
            dst_ref=X.at[h, pl.ds(0, rows), pl.ds(lo, n)],
            send_sem=p3s.at[part],
            recv_sem=p3r.at[h, part],
            device_id=(r, lax.rem(i + 1, E)),
            device_id_type=MESH,
        )

    def p3_wait(h):
        for part in range(NP):
            @pl.when(core == h)
            def _():
                p3_rows(h, part, ROWS - BLK).wait_recv()

            @pl.when(core != h)
            def _():
                p3_rows(h, part, ROWS).wait_recv()

    def p8_copy(h, p):
        return pltpu.make_async_remote_copy(
            src_ref=OUT.at[h, pl.ds(pl.multiple_of(p * BLK, BLK), BLK)],
            dst_ref=B.at[i],
            send_sem=p8s.at[h],
            recv_sem=p8r,
            device_id=(r, 2 * p + h),
            device_id_type=MESH,
        )

    def p8_wait():
        pltpu.make_async_remote_copy(
            src_ref=B.at[pl.ds(0, E - 1)],
            dst_ref=B.at[pl.ds(0, E - 1)],
            send_sem=p8s.at[0],
            recv_sem=p8r,
            device_id=(r, lax.rem(i + 1, E)),
            device_id_type=MESH,
        ).wait_recv()

    def p8_sent(h, rows):
        return pltpu.make_async_remote_copy(
            src_ref=OUT.at[h, pl.ds(0, rows)],
            dst_ref=OUT.at[h, pl.ds(0, rows)],
            send_sem=p8s.at[h],
            recv_sem=p8r,
            device_id=(r, lax.rem(i + 1, E)),
            device_id_type=MESH,
        )

    def group(owner):
        return lax.rem(owner + i, Z)

    def chunk(owner):
        return pl.ds(pl.multiple_of(group(owner) * CH, CH), CH)

    def piece(owner, sub):
        return pl.ds(pl.multiple_of(group(owner) * CH + sub * SUB, SUB), SUB)

    def up(h, owner):
        at = chunk(owner)

        @pl.loop(0, 4)
        def _(n):
            cols = pl.ds(pl.multiple_of(n * 512, 512), 512)
            PRE[h, at, cols] = jnp.dot(X[h, at, :], W[:, cols], preferred_element_type=jnp.float32)

    def up_part(h, q):
        @pl.loop(2 * q, 2 * q + 2)
        def _(n):
            cols = pl.ds(pl.multiple_of(n * 256, 256), 256)
            PRE[h, :, cols] = jnp.dot(X[h], W[:, cols], preferred_element_type=jnp.float32)

    def down(h, owner):
        at = chunk(owner)
        OUT[h, at, :] = jnp.dot(HD[h, at, :], DN[...], preferred_element_type=jnp.float32).astype(jnp.bfloat16)
        for j in range(CH // BLK):
            p = group(owner) * (CH // BLK) + j
            to = 2 * p + h

            @pl.when(to != i)
            def _():
                p8_copy(h, p).start()

            @pl.when(to == i)
            def _():
                B[i] = OUT[h, pl.ds(pl.multiple_of(pair * BLK, BLK), BLK), :]

    def rs_copy(h, way, sub, d):
        step = 1 if way == 0 else -1
        return pltpu.make_async_remote_copy(
            src_ref=RSS.at[h, way, sub, d - 1],
            dst_ref=RSR.at[h, way, sub, d - 1],
            send_sem=rss.at[h, way, sub, d - 1],
            recv_sem=rsr.at[h, way, sub, d - 1],
            device_id=(zdev(step), i),
            device_id_type=MESH,
        )

    def decode(h, way, sub, d):
        q = RSR[h, way, sub, d - 1]
        scale = jnp.exp2(q[:, 2 * FF:].astype(jnp.float32)) * (1.0 / LEVELS)
        return q, scale

    def rs_send(h, way, sub, d):
        owner = zdev(d if way == 0 else -d)
        far = FAR[h][way]
        s = PRE[h, piece(owner, sub), :]
        if d < far:
            rs_copy(h, way, sub, d + 1).wait_recv()
            q, scale = decode(h, way, sub, d + 1)
            s = s + q[:, :2 * FF].astype(jnp.float32) * jnp.tile(scale, (1, 16))
        most = jnp.maximum(jnp.max(jnp.abs(s), axis=1, keepdims=True), 1e-30)
        expo = jnp.ceil(jnp.log2(most))
        code = jnp.round(s * (jnp.exp2(-expo) * LEVELS))
        RSS[h, way, sub, d - 1, :, :2 * FF] = code.astype(jnp.int32).astype(jnp.int16)
        RSS[h, way, sub, d - 1, :, 2 * FF:] = jnp.broadcast_to(expo, (SUB, 128)).astype(jnp.int32).astype(jnp.int16)
        rs_copy(h, way, sub, d).start()

    def ag_copy(h, way, sub, k):
        step = 1 if way == 0 else -1
        origin = zdev(-(k - 1) * step)
        at = piece(origin, sub)
        return pltpu.make_async_remote_copy(
            src_ref=HD.at[h, at],
            dst_ref=HD.at[h, at],
            send_sem=ags.at[h, way, sub, k - 1],
            recv_sem=agr.at[h, way, sub, k - 1],
            device_id=(zdev(step), i),
            device_id_type=MESH,
        )

    def ag_wait(h, way, sub, k):
        step = 1 if way == 0 else -1
        origin = zdev(-k * step)
        at = piece(origin, sub)
        pltpu.make_async_remote_copy(
            src_ref=HD.at[h, at],
            dst_ref=HD.at[h, at],
            send_sem=ags.at[h, way, sub, k - 1],
            recv_sem=agr.at[h, way, sub, k - 1],
            device_id=(zdev(step), i),
            device_id_type=MESH,
        ).wait_recv()

    def finish(h, sub):
        at = piece(r, sub)
        s = PRE[h, at, :]
        for way in range(2):
            rs_copy(h, way, sub, 1).wait_recv()
            q, scale = decode(h, way, sub, 1)
            s = s + q[:, :2 * FF].astype(jnp.float32) * jnp.tile(scale, (1, 16))
        g = s[:, :FF]
        HD[h, at, :] = (g / (1.0 + jnp.exp(-g)) * s[:, FF:]).astype(jnp.bfloat16)
        for way in range(2):
            ag_copy(h, way, sub, 1).start()

    def ag_step(h, way, sub, k):
        ag_wait(h, way, sub, k)
        if k < FAR[h][way]:
            ag_copy(h, way, sub, k + 1).start()

    def combine():
        for zh in range(2):
            back = B[:, zh * HALF:(zh + 1) * HALF, :].reshape(ROWS, DS)
            CB[zh * 4 * TOK:(zh + 1) * 4 * TOK, :] = lax.dot_general(
                CT[zh], back, (((0,), (0,)), ((), ())), preferred_element_type=jnp.float32
            ).astype(jnp.bfloat16)

    mine = pl.ds(pl.multiple_of(r * DS, 128), DS)

    def p10_copy(k, part):
        c = zdev(k)
        lo, n = PARTS[part]
        return pltpu.make_async_remote_copy(
            src_ref=CB.at[pl.ds(pl.multiple_of(c * TOK, TOK), TOK), pl.ds(lo, n)],
            dst_ref=comb_out.at[:, pl.ds(pl.multiple_of(r * DS + lo, 128), n)],
            send_sem=p10s.at[c],
            recv_sem=p10r.at[r],
            device_id=(c, i),
            device_id_type=MESH,
        )

    def p10_all(k):
        c = zdev(k)
        return pltpu.make_async_remote_copy(
            src_ref=CB.at[pl.ds(pl.multiple_of(c * TOK, TOK), TOK)],
            dst_ref=comb_out.at[:, pl.ds(pl.multiple_of(c * DS, 128), DS)],
            send_sem=p10s.at[c],
            recv_sem=p10r.at[c],
            device_id=(c, i),
            device_id_type=MESH,
        )

    def p10_self():
        return pltpu.make_async_copy(
            CB.at[pl.ds(pl.multiple_of(r * TOK, TOK), TOK)], comb_out.at[:, mine], loc.at[3]
        )

    def p10_send(h, first, last):
        @pl.when(core == h)
        def _():
            for k, part in PIECES[first:last]:
                p10_copy(k, part).start()

    def hessian():
        at = pl.ds(pl.multiple_of(r * 128, 128), 128)
        total = lax.dot_general(
            HD[0, :, at], HD[0], (((0,), (0,)), ((), ())), preferred_element_type=jnp.float32
        ) + lax.dot_general(
            HD[1, :, at], HD[1], (((0,), (0,)), ((), ())), preferred_element_type=jnp.float32
        )
        hess_out[...] = total * (2.0 / 1024.0)

    def layout(first, last):
        @pl.loop(first, last)
        def _(n):
            at = pl.ds(pl.multiple_of(n * 64, 64), 64)
            W[at, :FF] = W3V[at, 0, :]
            W[at, FF:] = W3V[at, 1, :]

    def ag(h, k, sub):
        for way in range(2):
            if k <= FAR[h][way]:
                ag_step(h, way, sub, k)

    def downs(h, k):
        for way in range(2):
            if k <= FAR[h][way]:
                down(h, zdev(-k if way == 0 else k))

    def hand_in(part, h):
        @pl.when(core == h)
        def _():
            p1_wait(part)
            gather(part)
            if h == 0:
                p3_send(part)

    def hand_out(h):
        @pl.when(core == h)
        def _():
            p8_wait()
            combine()
            p10_self().start()

    meta_send()

    @pl.when(core == 0)
    def _():
        p1_send()

    w_copy.wait()
    layout(0, 8)
    own_copy.wait()
    meta_wait()
    routes()
    hand_in(0, 0)

    @pl.when(core == 0)
    def _():
        pl.semaphore_signal(go, inc=1, device_id=(r, i + 1), device_id_type=MESH)

    @pl.when(core == 1)
    def _():
        pl.semaphore_wait(go, 1)
        p1_send()

    for part in range(1, NP):
        hand_in(part, 0)
    layout(8, 14)
    for part in range(NP - 1):
        hand_in(part, 1)
    p3_wait(0)

    @pl.when(core == 1)
    def _():
        for part in range(NP - 1):
            p3_send(part)

    up(0, zdev(4))
    for sub in range(NSUB):
        rs_send(0, 0, sub, 4)
    up(0, zdev(-3))
    for sub in range(NSUB):
        rs_send(0, 1, sub, 3)
    hand_in(NP - 1, 1)

    @pl.when(core == 1)
    def _():
        p3_send(NP - 1)

    for q in range(4):
        up_part(0, q)
    for d in (3, 2):
        for sub in range(NSUB):
            rs_send(0, 0, sub, d)
            rs_send(0, 1, sub, d - 1)
    dn_copy.wait()
    p3_wait(1)
    up(1, zdev(-4))
    for sub in range(NSUB):
        rs_send(1, 1, sub, 4)
        rs_send(0, 0, sub, 1)
    for q in range(4):
        up_part(1, q)
    for sub in range(NSUB):
        finish(0, sub)
        rs_send(1, 0, sub, 3)
        rs_send(1, 1, sub, 3)
    down(0, r)
    ag(0, 1, 0)
    rs_send(1, 0, 0, 2)
    rs_send(1, 1, 0, 2)
    ag(0, 1, 1)
    ag(0, 2, 0)
    downs(0, 1)
    rs_send(1, 0, 1, 2)
    rs_send(1, 1, 1, 2)
    ag(0, 2, 1)
    ag(0, 3, 0)
    downs(0, 2)
    rs_send(1, 0, 0, 1)
    rs_send(1, 1, 0, 1)
    ag(0, 3, 1)
    ag(0, 4, 0)
    downs(0, 3)
    rs_send(1, 0, 1, 1)
    rs_send(1, 1, 1, 1)
    ag(0, 4, 1)
    downs(0, 4)
    for sub in range(NSUB):
        finish(1, sub)
    down(1, r)
    for sub in range(NSUB):
        ag(1, 1, sub)
    downs(1, 1)
    hand_out(0)
    p10_send(0, 0, 2)
    ag(1, 2, 0)
    p10_send(0, 2, 4)
    ag(1, 2, 1)
    p10_send(0, 4, 6)
    downs(1, 2)
    ag(1, 3, 0)
    p10_send(0, 6, 8)
    ag(1, 3, 1)
    p10_send(0, 8, 28)
    downs(1, 3)
    for sub in range(NSUB):
        ag(1, 4, sub)
    downs(1, 4)
    hessian()
    hand_out(1)
    p10_send(1, 0, 28)

    @pl.loop(1, Z)
    def _(k):
        for part in range(NP):
            tok_copy(k, part).wait_send()
        meta_copy(k).wait_send()
        p10_all(k).wait_send()
        p10_all(k).wait_recv()

    p10_self().wait()
    for part in range(NP):
        p3_sent(part).wait_send()

    for h in range(2):
        @pl.when(core == h)
        def _():
            p8_sent(h, ROWS - BLK).wait_send()

        @pl.when(core != h)
        def _():
            p8_sent(h, ROWS).wait_send()

        for way in range(2):
            for sub in range(NSUB):
                for d in range(1, FAR[h][way] + 1):
                    rs_copy(h, way, sub, d).wait_send()
                    ag_copy(h, way, sub, d).wait_send()


def local(tokens, expert_ids, combine_weights, gate_up_weight, down_weight):
    bf, f32 = jnp.bfloat16, jnp.float32
    dma = pltpu.SemaphoreType.DMA
    comb, hess = pl.pallas_call(
        kernel,
        out_shape=(
            jax.ShapeDtypeStruct((TOK, D), bf),
            jax.ShapeDtypeStruct((128, FF), f32),
        ),
        in_specs=[
            pl.BlockSpec(memory_space=pl.ANY),
            pl.BlockSpec(memory_space=pltpu.VMEM),
            pl.BlockSpec(memory_space=pltpu.VMEM),
            pl.BlockSpec(memory_space=pl.ANY),
            pl.BlockSpec(memory_space=pl.ANY),
        ],
        out_specs=(
            pl.BlockSpec(memory_space=pl.ANY),
            pl.BlockSpec(memory_space=pltpu.VMEM),
        ),
        scratch_shapes=[
            pltpu.VMEM((8, 128), f32),
            pltpu.VMEM((2, 4 * TOK, DS), bf),
            pltpu.VMEM((2, 4, 8, 128), f32),
            pltpu.VMEM((2, ROWS, 4 * TOK), bf),
            pltpu.VMEM((2, ROWS, 4 * TOK), bf),
            pltpu.VMEM((E, BLK, DS), bf),
            pltpu.VMEM((2, ROWS, DS), bf),
            pltpu.VMEM((DS, 2, FF), bf),
            pltpu.VMEM((DS, 2 * FF), bf),
            pltpu.VMEM((FF, DS), bf),
            pltpu.VMEM((2, ROWS, 2 * FF), f32),
            pltpu.VMEM((2, 2, NSUB, 4, SUB, MSG), jnp.int16),
            pltpu.VMEM((2, 2, NSUB, 4, SUB, MSG), jnp.int16),
            pltpu.VMEM((2, ROWS, FF), bf),
            pltpu.VMEM((2, ROWS, DS), bf),
            pltpu.VMEM((E, BLK, DS), bf),
            pltpu.VMEM((Z * TOK, DS), bf),
            pltpu.SemaphoreType.REGULAR,
            dma((4,)),
            dma((Z, NP)),
            dma((Z, NP)),
            dma((Z,)),
            dma((Z,)),
            dma((NP,)),
            dma((2, NP)),
            dma((2, 2, NSUB, 4)),
            dma((2, 2, NSUB, 4)),
            dma((2, 2, NSUB, 4)),
            dma((2, 2, NSUB, 4)),
            dma((2,)),
            dma,
            dma((Z,)),
            dma((Z,)),
        ],
        compiler_params=pltpu.CompilerParams(
            collective_id=0, has_side_effects=True, vmem_limit_bytes=60 * 1024 * 1024
        ),
        name="moe",
    )(tokens, expert_ids.T, combine_weights.T, gate_up_weight[0], down_weight[0])
    return comb.astype(jnp.float32), hess[None]


def solution(mesh):
    return jax.shard_map(
        local,
        mesh=mesh,
        in_specs=(
            P(("rep", "exp"), None),
            P(("rep", "exp"), None),
            P(("rep", "exp"), None),
            P("exp", "rep", None, None),
            P("exp", None, "rep"),
        ),
        out_specs=(P(("rep", "exp"), None), P("exp", "rep", None)),
        check_vma=False,
    )
```

```python
import functools

import jax
import jax.numpy as jnp
from jax import lax
from jax.experimental import pallas as pl
from jax.experimental.pallas import tpu as pltpu
from jax.sharding import PartitionSpec as P

MESH = pl.DeviceIdType.MESH
Z = 8
E = 32
TOK = 64
SLOT = 4
D = 7168
DS = D // Z
FF = 1024
ROWS = 512
HALF = 16
BLK = 32
CH = ROWS // Z
NSUB = 2
SUB = CH // NSUB
MSG = 2 * FF + 128
LEVELS = 32000.0
FAR = ((4, 3), (3, 4))
PARTS = ((0, 128), (128, 256), (384, 256), (640, 256))
NP = len(PARTS)
PIECES = [(q, part) for part in range(NP) for q in range(4)]


def kernel(
    tok, ids, wts, w3, dn, comb_out, hess_out,
    META, T, M, MS, DM, CT, G, X, W3V, W, DN, PRE, RSS, RSR, HD, OUT, B, CB,
    go, sibs, sibr, loc, p1s, p1r, m1s, m1r, p3s, p3r, rss, rsr, ags, agr, p8s, p8r, p10s, p10r,
):
    r = lax.axis_index("rep")
    i = lax.axis_index("exp")
    core = lax.rem(i, 2)
    pair = i // 2
    sib = i + 1 - 2 * core
    zh_own, cl_own = lax.rem(r, 2), r // 2

    def zdev(k):
        return lax.rem(r + k + Z, Z)

    w_copy = pltpu.make_async_copy(w3, W3V, loc.at[0])
    dn_copy = pltpu.make_async_copy(dn, DN, loc.at[1])
    own_copy = pltpu.make_async_copy(
        tok.at[:, pl.ds(pl.multiple_of(r * DS, 128), DS)],
        T.at[zh_own, pl.ds(pl.multiple_of(cl_own * TOK, TOK), TOK)],
        loc.at[2],
    )
    own_copy.start()
    w_copy.start()
    dn_copy.start()

    barrier = pltpu.get_barrier_semaphore()

    @pl.loop(1, Z)
    def _(k):
        pl.semaphore_signal(barrier, inc=1, device_id=(zdev(k), i), device_id_type=MESH)
        pl.semaphore_signal(barrier, inc=1, device_id=(zdev(k), sib), device_id_type=MESH)

    @pl.loop(1, E)
    def _(k):
        pl.semaphore_signal(barrier, inc=1, device_id=(r, lax.rem(i + k, E)), device_id_type=MESH)

    pl.semaphore_wait(barrier, 2 * (Z - 1) + E - 1)

    def tok_copy(k, part):
        to = zdev(k)
        lo, n = PARTS[part]
        return pltpu.make_async_remote_copy(
            src_ref=tok.at[:, pl.ds(pl.multiple_of(to * DS + lo, 128), n)],
            dst_ref=T.at[zh_own, pl.ds(pl.multiple_of(cl_own * TOK, TOK), TOK), pl.ds(lo, n)],
            send_sem=p1s.at[k, part],
            recv_sem=p1r.at[r, part],
            device_id=(to, i),
            device_id_type=MESH,
        )

    def meta_copy(k):
        return pltpu.make_async_remote_copy(
            src_ref=META,
            dst_ref=M.at[zh_own, cl_own],
            send_sem=m1s.at[k],
            recv_sem=m1r.at[r],
            device_id=(zdev(k), i),
            device_id_type=MESH,
        )

    def p1_send():
        for part in range(NP):
            @pl.loop(1, Z)
            def _(k):
                tok_copy(k, part).start()

    def meta_send():
        row = ids[...].astype(jnp.float32)
        row = jnp.concatenate([row[0:1, :], row[1:2, :]], axis=1)
        hot = lax.broadcasted_iota(jnp.int32, (E, 2 * TOK), 0).astype(jnp.float32) == row
        hot = jnp.where(hot, 1.0, 0.0)
        earlier = lax.broadcasted_iota(jnp.int32, (2 * TOK, 2 * TOK), 0) < lax.broadcasted_iota(
            jnp.int32, (2 * TOK, 2 * TOK), 1
        )
        count = jnp.dot(
            hot.astype(jnp.bfloat16),
            jnp.where(earlier, 1.0, 0.0).astype(jnp.bfloat16),
            preferred_element_type=jnp.float32,
        )
        rank = jnp.sum(hot * count, axis=0, keepdims=True)
        pos = row * HALF + rank + (cl_own * SLOT).astype(jnp.float32)
        w = wts[...].astype(jnp.float32)
        four = jnp.concatenate([pos[:, :TOK], pos[:, TOK:], w], axis=0)
        fill = jnp.where(lax.broadcasted_iota(jnp.int32, (4, TOK), 0) < 2, -1.0, 0.0)
        wide = jnp.where(
            lax.rem(cl_own, 2) == 0,
            jnp.concatenate([four, fill], axis=1),
            jnp.concatenate([fill, four], axis=1),
        )
        META[...] = jnp.concatenate([wide, wide], axis=0)
        M[zh_own, cl_own] = jnp.concatenate([wide, wide], axis=0)

        @pl.loop(1, Z)
        def _(k):
            meta_copy(k).start()

    def meta_wait():
        @pl.loop(1, Z)
        def _(k):
            c = zdev(k)
            pltpu.make_async_remote_copy(
                src_ref=META,
                dst_ref=M.at[lax.rem(c, 2), c // 2],
                send_sem=m1s.at[k],
                recv_sem=m1r.at[c],
                device_id=(c, i),
                device_id_type=MESH,
            ).wait_recv()

    def p1_wait(part):
        lo, n = PARTS[part]

        @pl.loop(1, Z)
        def _(k):
            c = zdev(k)
            at = pl.ds(pl.multiple_of((c // 2) * TOK, TOK), TOK)
            zh = lax.rem(c, 2)
            pltpu.make_async_remote_copy(
                src_ref=T.at[zh, at, pl.ds(lo, n)],
                dst_ref=T.at[zh, at, pl.ds(lo, n)],
                send_sem=p1s.at[k, part],
                recv_sem=p1r.at[c, part],
                device_id=(c, i),
                device_id_type=MESH,
            ).wait_recv()

    sib_copy = pltpu.make_async_remote_copy(
        src_ref=M.at[1], dst_ref=MS, send_sem=sibs, recv_sem=sibr, device_id=(r, sib), device_id_type=MESH
    )

    def hits(m):
        rows = lax.broadcasted_iota(jnp.int32, (ROWS, 128), 0).astype(jnp.float32)
        return rows == m[0:1, :], rows == m[1:2, :]

    def weights(which, p, m):
        hit0, hit1 = hits(m)
        CT[which, :, p * 128:(p + 1) * 128] = (
            jnp.where(hit0, m[2:3, :], 0.0) + jnp.where(hit1, m[3:4, :], 0.0)
        ).astype(jnp.bfloat16)

    def routes():
        sib_copy.start()
        for p in range(2):
            for zh in range(2):
                m = jnp.maximum(M[zh, 2 * p], M[zh, 2 * p + 1])
                hit0, hit1 = hits(m)
                DM[zh, :, p * 128:(p + 1) * 128] = jnp.where(hit0 | hit1, 1.0, 0.0).astype(jnp.bfloat16)

    def returns():
        sib_copy.wait_recv()
        for p in range(2):
            weights(0, p, jnp.maximum(M[0, 2 * p], M[0, 2 * p + 1]))
            weights(1, p, jnp.maximum(MS[2 * p], MS[2 * p + 1]))

    def gather(part):
        lo, n = PARTS[part]
        for zh in range(2):
            @pl.loop(0, 4)
            def _(q):
                at = pl.ds(pl.multiple_of(q * 128, 128), 128)
                got = jnp.dot(DM[zh, at, :], T[zh, :, lo:lo + n], preferred_element_type=jnp.float32)
                G[pl.ds(q * 8, 8), zh * HALF:(zh + 1) * HALF, lo:lo + n] = got.astype(jnp.bfloat16).reshape(8, HALF, n)

    def p3_copy(part, k):
        to = lax.rem(i + k, E)
        lo, n = PARTS[part]
        return pltpu.make_async_remote_copy(
            src_ref=G.at[to, :, pl.ds(lo, n)],
            dst_ref=X.at[core, pl.ds(pl.multiple_of(pair * BLK, BLK), BLK), pl.ds(lo, n)],
            send_sem=p3s.at[part],
            recv_sem=p3r.at[core, part],
            device_id=(r, to),
            device_id_type=MESH,
        )

    def p3_send(part):
        @pl.loop(1, E)
        def _(k):
            p3_copy(part, k).start()

        lo, n = PARTS[part]
        X[core, pl.ds(pl.multiple_of(pair * BLK, BLK), BLK), lo:lo + n] = G[i, :, lo:lo + n]

    def p3_sent(part):
        lo, n = PARTS[part]
        return pltpu.make_async_remote_copy(
            src_ref=G.at[pl.ds(0, E - 1), :, pl.ds(lo, n)],
            dst_ref=G.at[pl.ds(0, E - 1), :, pl.ds(lo, n)],
            send_sem=p3s.at[part],
            recv_sem=p3r.at[0, part],
            device_id=(r, lax.rem(i + 1, E)),
            device_id_type=MESH,
        )

    def p3_rows(h, part, rows):
        lo, n = PARTS[part]
        return pltpu.make_async_remote_copy(
            src_ref=X.at[h, pl.ds(0, rows), pl.ds(lo, n)],
            dst_ref=X.at[h, pl.ds(0, rows), pl.ds(lo, n)],
            send_sem=p3s.at[part],
            recv_sem=p3r.at[h, part],
            device_id=(r, lax.rem(i + 1, E)),
            device_id_type=MESH,
        )

    def p3_wait(h):
        for part in range(NP):
            @pl.when(core == h)
            def _():
                p3_rows(h, part, ROWS - BLK).wait_recv()

            @pl.when(core != h)
            def _():
                p3_rows(h, part, ROWS).wait_recv()

    def p8_copy(h, p, zh):
        return pltpu.make_async_remote_copy(
            src_ref=OUT.at[h, pl.ds(pl.multiple_of(p * BLK + zh * HALF, HALF), HALF)],
            dst_ref=B.at[h, i],
            send_sem=p8s.at[h],
            recv_sem=p8r.at[h],
            device_id=(r, 2 * p + (h if zh == 0 else 1 - h)),
            device_id_type=MESH,
        )

    def p8_wait(h):
        pltpu.make_async_remote_copy(
            src_ref=B.at[h, pl.ds(0, E - 1)],
            dst_ref=B.at[h, pl.ds(0, E - 1)],
            send_sem=p8s.at[h],
            recv_sem=p8r.at[h],
            device_id=(r, sib),
            device_id_type=MESH,
        ).wait_recv()

    def p8_sent(h):
        most = pl.ds(0, (E - 1) * HALF)
        return pltpu.make_async_remote_copy(
            src_ref=OUT.at[h, most],
            dst_ref=OUT.at[h, most],
            send_sem=p8s.at[h],
            recv_sem=p8r.at[h],
            device_id=(r, sib),
            device_id_type=MESH,
        )

    def group(owner):
        return lax.rem(owner + i, Z)

    def chunk(owner):
        return pl.ds(pl.multiple_of(group(owner) * CH, CH), CH)

    def piece(owner, sub):
        return pl.ds(pl.multiple_of(group(owner) * CH + sub * SUB, SUB), SUB)

    def up(h, owner):
        at = chunk(owner)

        @pl.loop(0, 4)
        def _(n):
            cols = pl.ds(pl.multiple_of(n * 512, 512), 512)
            PRE[h, at, cols] = jnp.dot(X[h, at, :], W[:, cols], preferred_element_type=jnp.float32)

    def up_two(h, first, second):
        one, two = chunk(first), chunk(second)

        @pl.loop(0, 4)
        def _(n):
            cols = pl.ds(pl.multiple_of(n * 512, 512), 512)
            rows = jnp.concatenate([X[h, one, :], X[h, two, :]], axis=0)
            got = jnp.dot(rows, W[:, cols], preferred_element_type=jnp.float32)
            PRE[h, one, cols] = got[:CH]
            PRE[h, two, cols] = got[CH:]

    def up_part(h, q):
        @pl.loop(2 * q, 2 * q + 2)
        def _(n):
            cols = pl.ds(pl.multiple_of(n * 256, 256), 256)
            PRE[h, :, cols] = jnp.dot(X[h], W[:, cols], preferred_element_type=jnp.float32)

    def down(h, owner):
        at = chunk(owner)
        OUT[h, at, :] = jnp.dot(HD[h, at, :], DN[...], preferred_element_type=jnp.float32).astype(jnp.bfloat16)
        for j in range(CH // BLK):
            p = group(owner) * (CH // BLK) + j
            for zh in range(2):
                to = 2 * p + (h if zh == 0 else 1 - h)

                @pl.when(to != i)
                def _():
                    p8_copy(h, p, zh).start()

                @pl.when(to == i)
                def _():
                    B[h, i] = OUT[h, pl.ds(pl.multiple_of(pair * BLK + zh * HALF, HALF), HALF), :]

    def rs_copy(h, way, sub, d):
        step = 1 if way == 0 else -1
        return pltpu.make_async_remote_copy(
            src_ref=RSS.at[h, way, sub, d - 1],
            dst_ref=RSR.at[h, way, sub, d - 1],
            send_sem=rss.at[h, way, sub, d - 1],
            recv_sem=rsr.at[h, way, sub, d - 1],
            device_id=(zdev(step), i),
            device_id_type=MESH,
        )

    def decode(h, way, sub, d):
        q = RSR[h, way, sub, d - 1]
        scale = jnp.exp2(q[:, 2 * FF:].astype(jnp.float32)) * (1.0 / LEVELS)
        return q, scale

    def rs_send(h, way, sub, d):
        owner = zdev(d if way == 0 else -d)
        far = FAR[h][way]
        s = PRE[h, piece(owner, sub), :]
        if d < far:
            rs_copy(h, way, sub, d + 1).wait_recv()
            q, scale = decode(h, way, sub, d + 1)
            s = s + q[:, :2 * FF].astype(jnp.float32) * jnp.tile(scale, (1, 16))
        most = jnp.maximum(jnp.max(jnp.abs(s), axis=1, keepdims=True), 1e-30)
        expo = jnp.ceil(jnp.log2(most))
        code = jnp.round(s * (jnp.exp2(-expo) * LEVELS))
        RSS[h, way, sub, d - 1, :, :2 * FF] = code.astype(jnp.int32).astype(jnp.int16)
        RSS[h, way, sub, d - 1, :, 2 * FF:] = jnp.broadcast_to(expo, (SUB, 128)).astype(jnp.int32).astype(jnp.int16)
        rs_copy(h, way, sub, d).start()

    def ag_copy(h, way, sub, k):
        step = 1 if way == 0 else -1
        origin = zdev(-(k - 1) * step)
        at = piece(origin, sub)
        return pltpu.make_async_remote_copy(
            src_ref=HD.at[h, at],
            dst_ref=HD.at[h, at],
            send_sem=ags.at[h, way, sub, k - 1],
            recv_sem=agr.at[h, way, sub, k - 1],
            device_id=(zdev(step), i),
            device_id_type=MESH,
        )

    def ag_wait(h, way, sub, k):
        step = 1 if way == 0 else -1
        origin = zdev(-k * step)
        at = piece(origin, sub)
        pltpu.make_async_remote_copy(
            src_ref=HD.at[h, at],
            dst_ref=HD.at[h, at],
            send_sem=ags.at[h, way, sub, k - 1],
            recv_sem=agr.at[h, way, sub, k - 1],
            device_id=(zdev(step), i),
            device_id_type=MESH,
        ).wait_recv()

    def finish(h, sub):
        at = piece(r, sub)
        s = PRE[h, at, :]
        for way in range(2):
            rs_copy(h, way, sub, 1).wait_recv()
            q, scale = decode(h, way, sub, 1)
            s = s + q[:, :2 * FF].astype(jnp.float32) * jnp.tile(scale, (1, 16))
        g = s[:, :FF]
        HD[h, at, :] = (g / (1.0 + jnp.exp(-g)) * s[:, FF:]).astype(jnp.bfloat16)
        for way in range(2):
            ag_copy(h, way, sub, 1).start()

    def ag_step(h, way, sub, k):
        ag_wait(h, way, sub, k)
        if k < FAR[h][way]:
            ag_copy(h, way, sub, k + 1).start()

    def whose(h):
        return lax.rem(core + h, 2)

    def combine(h):
        CB[h] = lax.dot_general(
            CT[whose(h)], B[h].reshape(ROWS, DS), (((0,), (0,)), ((), ())), preferred_element_type=jnp.float32
        ).astype(jnp.bfloat16)

    mine = pl.ds(pl.multiple_of(r * DS, 128), DS)

    def p10_copy(h, q, part):
        w = whose(h)
        cl = lax.rem(q + r // 2, 4)
        lo, n = PARTS[part]
        return pltpu.make_async_remote_copy(
            src_ref=CB.at[h, pl.ds(pl.multiple_of(cl * TOK, TOK), TOK), pl.ds(lo, n)],
            dst_ref=comb_out.at[:, pl.ds(pl.multiple_of(r * DS + lo, 128), n)],
            send_sem=p10s.at[h, cl],
            recv_sem=p10r.at[r],
            device_id=(2 * cl + w, i + w * (sib - i)),
            device_id_type=MESH,
        )

    def p10_away(h, q):
        w = whose(h)
        cl = lax.rem(q + r // 2, 4)
        return jnp.logical_or(w == 1, 2 * cl + w != r)

    def p10_self():
        return pltpu.make_async_copy(
            CB.at[core, pl.ds(pl.multiple_of((r // 2) * TOK, TOK), TOK)], comb_out.at[:, mine], loc.at[3]
        )

    def p10_send(h, first, last):
        for q, part in PIECES[first:last]:
            @pl.when(p10_away(h, q))
            def _():
                p10_copy(h, q, part).start()

    def hessian():
        at = pl.ds(pl.multiple_of(r * 128, 128), 128)
        total = lax.dot_general(
            HD[0, :, at], HD[0], (((0,), (0,)), ((), ())), preferred_element_type=jnp.float32
        ) + lax.dot_general(
            HD[1, :, at], HD[1], (((0,), (0,)), ((), ())), preferred_element_type=jnp.float32
        )
        hess_out[...] = total * (2.0 / 1024.0)

    def layout(first, last):
        @pl.loop(first, last)
        def _(n):
            at = pl.ds(pl.multiple_of(n * 64, 64), 64)
            W[at, :FF] = W3V[at, 0, :]
            W[at, FF:] = W3V[at, 1, :]

    def ag(h, k, sub):
        for way in range(2):
            if k <= FAR[h][way]:
                ag_step(h, way, sub, k)

    def downs(h, k):
        for way in range(2):
            if k <= FAR[h][way]:
                down(h, zdev(-k if way == 0 else k))

    def hand_in(part, h):
        @pl.when(core == h)
        def _():
            p1_wait(part)
            gather(part)
            if h == 0:
                p3_send(part)

    def hand_out(h):
        p8_wait(h)
        combine(h)

        @pl.when(jnp.logical_and(core == h, lax.rem(r, 2) == 0))
        def _():
            p10_self().start()

    meta_send()

    @pl.when(core == 0)
    def _():
        p1_send()

    w_copy.wait()
    layout(0, 8)
    own_copy.wait()
    meta_wait()
    routes()
    hand_in(0, 0)
    hand_in(1, 0)

    @pl.when(core == 0)
    def _():
        pl.semaphore_signal(go, inc=1, device_id=(r, i + 1), device_id_type=MESH)

    @pl.when(core == 1)
    def _():
        pl.semaphore_wait(go, 1)
        p1_send()

    for part in range(2, NP):
        hand_in(part, 0)
    returns()
    layout(8, 14)
    for part in range(NP - 1):
        hand_in(part, 1)
    p3_wait(0)

    @pl.when(core == 1)
    def _():
        for part in range(NP - 1):
            p3_send(part)

    up_two(0, zdev(4), zdev(-3))
    for sub in range(NSUB):
        rs_send(0, 0, sub, 4)
        rs_send(0, 1, sub, 3)
    hand_in(NP - 1, 1)

    @pl.when(core == 1)
    def _():
        p3_send(NP - 1)

    for q in range(4):
        up_part(0, q)
    for d in (3, 2):
        for sub in range(NSUB):
            rs_send(0, 0, sub, d)
            rs_send(0, 1, sub, d - 1)
    dn_copy.wait()
    p3_wait(1)
    up(1, zdev(-4))
    for sub in range(NSUB):
        rs_send(1, 1, sub, 4)
        rs_send(0, 0, sub, 1)
    for q in range(4):
        up_part(1, q)
    for sub in range(NSUB):
        finish(0, sub)
        rs_send(1, 0, sub, 3)
        rs_send(1, 1, sub, 3)
    down(0, r)
    ag(0, 1, 0)
    rs_send(1, 0, 0, 2)
    rs_send(1, 1, 0, 2)
    ag(0, 1, 1)
    ag(0, 2, 0)
    downs(0, 1)
    rs_send(1, 0, 1, 2)
    rs_send(1, 1, 1, 2)
    ag(0, 2, 1)
    ag(0, 3, 0)
    downs(0, 2)
    rs_send(1, 0, 0, 1)
    rs_send(1, 1, 0, 1)
    ag(0, 3, 1)
    ag(0, 4, 0)
    downs(0, 3)
    rs_send(1, 0, 1, 1)
    rs_send(1, 1, 1, 1)
    ag(0, 4, 1)
    downs(0, 4)
    for sub in range(NSUB):
        finish(1, sub)
    down(1, r)
    for sub in range(NSUB):
        ag(1, 1, sub)
    downs(1, 1)
    ag(1, 2, 0)
    ag(1, 2, 1)
    downs(1, 2)
    ag(1, 3, 0)
    ag(1, 3, 1)
    hand_out(0)
    p10_send(0, 0, 6)
    downs(1, 3)
    for sub in range(NSUB):
        ag(1, 4, sub)
    downs(1, 4)
    p10_send(0, 6, 16)
    hessian()
    hand_out(1)
    p10_send(1, 0, 16)

    @pl.loop(1, Z)
    def _(k):
        for part in range(NP):
            tok_copy(k, part).wait_send()
        meta_copy(k).wait_send()

    sib_copy.wait_send()
    for part in range(NP):
        p3_sent(part).wait_send()

    for h in range(2):
        p8_sent(h).wait_send()
        for way in range(2):
            for sub in range(NSUB):
                for d in range(1, FAR[h][way] + 1):
                    rs_copy(h, way, sub, d).wait_send()
                    ag_copy(h, way, sub, d).wait_send()
        for q in range(4):
            cl = lax.rem(q + r // 2, 4)

            @pl.when(p10_away(h, q))
            def _():
                pltpu.make_async_remote_copy(
                    src_ref=CB.at[h, pl.ds(pl.multiple_of(cl * TOK, TOK), TOK)],
                    dst_ref=comb_out.at[:, mine],
                    send_sem=p10s.at[h, cl],
                    recv_sem=p10r.at[r],
                    device_id=(r, sib),
                    device_id_type=MESH,
                ).wait_send()

    @pl.when(lax.rem(r, 2) == 0)
    def _():
        p10_self().wait()

    @pl.loop(0, Z)
    def _(k):
        c = zdev(k)

        @pl.when(jnp.logical_or(lax.rem(r, 2) == 1, k != 0))
        def _():
            pltpu.make_async_remote_copy(
                src_ref=CB.at[0, pl.ds(0, TOK)],
                dst_ref=comb_out.at[:, pl.ds(pl.multiple_of(c * DS, 128), DS)],
                send_sem=p10s.at[0, 0],
                recv_sem=p10r.at[c],
                device_id=(r, sib),
                device_id_type=MESH,
            ).wait_recv()


def local(tokens, expert_ids, combine_weights, gate_up_weight, down_weight):
    bf, f32 = jnp.bfloat16, jnp.float32
    dma = pltpu.SemaphoreType.DMA
    comb, hess = pl.pallas_call(
        kernel,
        out_shape=(
            jax.ShapeDtypeStruct((TOK, D), bf),
            jax.ShapeDtypeStruct((128, FF), f32),
        ),
        in_specs=[
            pl.BlockSpec(memory_space=pl.ANY),
            pl.BlockSpec(memory_space=pltpu.VMEM),
            pl.BlockSpec(memory_space=pltpu.VMEM),
            pl.BlockSpec(memory_space=pl.ANY),
            pl.BlockSpec(memory_space=pl.ANY),
        ],
        out_specs=(
            pl.BlockSpec(memory_space=pl.ANY),
            pl.BlockSpec(memory_space=pltpu.VMEM),
        ),
        scratch_shapes=[
            pltpu.VMEM((8, 128), f32),
            pltpu.VMEM((2, 4 * TOK, DS), bf),
            pltpu.VMEM((2, 4, 8, 128), f32),
            pltpu.VMEM((4, 8, 128), f32),
            pltpu.VMEM((2, ROWS, 4 * TOK), bf),
            pltpu.VMEM((2, ROWS, 4 * TOK), bf),
            pltpu.VMEM((E, BLK, DS), bf),
            pltpu.VMEM((2, ROWS, DS), bf),
            pltpu.VMEM((DS, 2, FF), bf),
            pltpu.VMEM((DS, 2 * FF), bf),
            pltpu.VMEM((FF, DS), bf),
            pltpu.VMEM((2, ROWS, 2 * FF), f32),
            pltpu.VMEM((2, 2, NSUB, 4, SUB, MSG), jnp.int16),
            pltpu.VMEM((2, 2, NSUB, 4, SUB, MSG), jnp.int16),
            pltpu.VMEM((2, ROWS, FF), bf),
            pltpu.VMEM((2, ROWS, DS), bf),
            pltpu.VMEM((2, E, HALF, DS), bf),
            pltpu.VMEM((2, 4 * TOK, DS), bf),
            pltpu.SemaphoreType.REGULAR,
            dma,
            dma,
            dma((4,)),
            dma((Z, NP)),
            dma((Z, NP)),
            dma((Z,)),
            dma((Z,)),
            dma((NP,)),
            dma((2, NP)),
            dma((2, 2, NSUB, 4)),
            dma((2, 2, NSUB, 4)),
            dma((2, 2, NSUB, 4)),
            dma((2, 2, NSUB, 4)),
            dma((2,)),
            dma((2,)),
            dma((2, 4)),
            dma((Z,)),
        ],
        compiler_params=pltpu.CompilerParams(
            collective_id=0, has_side_effects=True, vmem_limit_bytes=60 * 1024 * 1024
        ),
        name="moe",
    )(tokens, expert_ids.T, combine_weights.T, gate_up_weight[0], down_weight[0])
    return comb.astype(jnp.float32), hess[None]


def solution(mesh):
    return jax.shard_map(
        local,
        mesh=mesh,
        in_specs=(
            P(("rep", "exp"), None),
            P(("rep", "exp"), None),
            P(("rep", "exp"), None),
            P("exp", "rep", None, None),
            P("exp", None, "rep"),
        ),
        out_specs=(P(("rep", "exp"), None), P("exp", "rep", None)),
        check_vma=False,
    )
```

```python
import functools

import jax
import jax.numpy as jnp
from jax import lax
from jax.experimental import pallas as pl
from jax.experimental.pallas import tpu as pltpu
from jax.sharding import PartitionSpec as P

MESH = pl.DeviceIdType.MESH
Z = 8
E = 32
TOK = 64
SLOT = 4
D = 7168
DS = D // Z
FF = 1024
ROWS = 512
HALF = 16
BLK = 32
CH = ROWS // Z
NSUB = 2
SUB = CH // NSUB
LANES = 2 * FF // 128
TILES = 2 * LANES + 1
LEVELS = 32000.0
FAR = ((4, 3), (3, 4))
PARTS = ((0, 128), (128, 256), (384, 256), (640, 256))
NP = len(PARTS)
PIECES = [(q, part) for part in range(NP) for q in range(4)]


def kernel(
    tok, ids, wts, w3, dn, comb_out, hess_out,
    META, T, M, MS, DM, CT, G, X, W3V, W, DN, PRE, RSS, RSR, HD, OUT, B, CB,
    go, sibs, sibr, loc, p1s, p1r, m1s, m1r, p3s, p3r, rss, rsr, ags, agr, p8s, p8r, p10s, p10r,
):
    r = lax.axis_index("rep")
    i = lax.axis_index("exp")
    core = lax.rem(i, 2)
    pair = i // 2
    sib = i + 1 - 2 * core
    zh_own, cl_own = lax.rem(r, 2), r // 2

    def zdev(k):
        return lax.rem(r + k + Z, Z)

    w_copy = pltpu.make_async_copy(w3, W3V, loc.at[0])
    dn_copy = pltpu.make_async_copy(dn, DN, loc.at[1])
    own_copy = pltpu.make_async_copy(
        tok.at[:, pl.ds(pl.multiple_of(r * DS, 128), DS)],
        T.at[zh_own, pl.ds(pl.multiple_of(cl_own * TOK, TOK), TOK)],
        loc.at[2],
    )
    own_copy.start()
    w_copy.start()
    dn_copy.start()

    barrier = pltpu.get_barrier_semaphore()

    @pl.loop(1, Z)
    def _(k):
        pl.semaphore_signal(barrier, inc=1, device_id=(zdev(k), i), device_id_type=MESH)
        pl.semaphore_signal(barrier, inc=1, device_id=(zdev(k), sib), device_id_type=MESH)

    @pl.loop(1, E)
    def _(k):
        pl.semaphore_signal(barrier, inc=1, device_id=(r, lax.rem(i + k, E)), device_id_type=MESH)

    pl.semaphore_wait(barrier, 2 * (Z - 1) + E - 1)

    def tok_copy(k, part):
        to = zdev(k)
        lo, n = PARTS[part]
        return pltpu.make_async_remote_copy(
            src_ref=tok.at[:, pl.ds(pl.multiple_of(to * DS + lo, 128), n)],
            dst_ref=T.at[zh_own, pl.ds(pl.multiple_of(cl_own * TOK, TOK), TOK), pl.ds(lo, n)],
            send_sem=p1s.at[k, part],
            recv_sem=p1r.at[r, part],
            device_id=(to, i),
            device_id_type=MESH,
        )

    def meta_copy(k):
        return pltpu.make_async_remote_copy(
            src_ref=META,
            dst_ref=M.at[zh_own, cl_own],
            send_sem=m1s.at[k],
            recv_sem=m1r.at[r],
            device_id=(zdev(k), i),
            device_id_type=MESH,
        )

    def p1_send():
        for part in range(NP):
            @pl.loop(1, Z)
            def _(k):
                tok_copy(k, part).start()

    def meta_send():
        row = ids[...].astype(jnp.float32)
        row = jnp.concatenate([row[0:1, :], row[1:2, :]], axis=1)
        hot = lax.broadcasted_iota(jnp.int32, (E, 2 * TOK), 0).astype(jnp.float32) == row
        hot = jnp.where(hot, 1.0, 0.0)
        earlier = lax.broadcasted_iota(jnp.int32, (2 * TOK, 2 * TOK), 0) < lax.broadcasted_iota(
            jnp.int32, (2 * TOK, 2 * TOK), 1
        )
        count = jnp.dot(
            hot.astype(jnp.bfloat16),
            jnp.where(earlier, 1.0, 0.0).astype(jnp.bfloat16),
            preferred_element_type=jnp.float32,
        )
        rank = jnp.sum(hot * count, axis=0, keepdims=True)
        pos = row * HALF + rank + (cl_own * SLOT).astype(jnp.float32)
        w = wts[...].astype(jnp.float32)
        four = jnp.concatenate([pos[:, :TOK], pos[:, TOK:], w], axis=0)
        fill = jnp.where(lax.broadcasted_iota(jnp.int32, (4, TOK), 0) < 2, -1.0, 0.0)
        wide = jnp.where(
            lax.rem(cl_own, 2) == 0,
            jnp.concatenate([four, fill], axis=1),
            jnp.concatenate([fill, four], axis=1),
        )
        META[...] = jnp.concatenate([wide, wide], axis=0)
        M[zh_own, cl_own] = jnp.concatenate([wide, wide], axis=0)

        @pl.loop(1, Z)
        def _(k):
            meta_copy(k).start()

    def meta_wait():
        @pl.loop(1, Z)
        def _(k):
            c = zdev(k)
            pltpu.make_async_remote_copy(
                src_ref=META,
                dst_ref=M.at[lax.rem(c, 2), c // 2],
                send_sem=m1s.at[k],
                recv_sem=m1r.at[c],
                device_id=(c, i),
                device_id_type=MESH,
            ).wait_recv()

    def p1_wait(part):
        lo, n = PARTS[part]

        @pl.loop(1, Z)
        def _(k):
            c = zdev(k)
            at = pl.ds(pl.multiple_of((c // 2) * TOK, TOK), TOK)
            zh = lax.rem(c, 2)
            pltpu.make_async_remote_copy(
                src_ref=T.at[zh, at, pl.ds(lo, n)],
                dst_ref=T.at[zh, at, pl.ds(lo, n)],
                send_sem=p1s.at[k, part],
                recv_sem=p1r.at[c, part],
                device_id=(c, i),
                device_id_type=MESH,
            ).wait_recv()

    sib_copy = pltpu.make_async_remote_copy(
        src_ref=M.at[1], dst_ref=MS, send_sem=sibs, recv_sem=sibr, device_id=(r, sib), device_id_type=MESH
    )

    def hits(m):
        rows = lax.broadcasted_iota(jnp.int32, (ROWS, 128), 0).astype(jnp.float32)
        return rows == m[0:1, :], rows == m[1:2, :]

    def weights(which, p, m):
        hit0, hit1 = hits(m)
        CT[which, :, p * 128:(p + 1) * 128] = (
            jnp.where(hit0, m[2:3, :], 0.0) + jnp.where(hit1, m[3:4, :], 0.0)
        ).astype(jnp.bfloat16)

    def routes():
        sib_copy.start()
        for p in range(2):
            for zh in range(2):
                m = jnp.maximum(M[zh, 2 * p], M[zh, 2 * p + 1])
                hit0, hit1 = hits(m)
                DM[zh, :, p * 128:(p + 1) * 128] = jnp.where(hit0 | hit1, 1.0, 0.0).astype(jnp.bfloat16)

    def returns():
        sib_copy.wait_recv()
        for p in range(2):
            weights(0, p, jnp.maximum(M[0, 2 * p], M[0, 2 * p + 1]))
            weights(1, p, jnp.maximum(MS[2 * p], MS[2 * p + 1]))

    def gather(part):
        lo, n = PARTS[part]
        for zh in range(2):
            @pl.loop(0, 4)
            def _(q):
                at = pl.ds(pl.multiple_of(q * 128, 128), 128)
                got = jnp.dot(DM[zh, at, :], T[zh, :, lo:lo + n], preferred_element_type=jnp.float32)
                G[pl.ds(q * 8, 8), zh * HALF:(zh + 1) * HALF, lo:lo + n] = got.astype(jnp.bfloat16).reshape(8, HALF, n)

    def p3_copy(part, k):
        to = lax.rem(i + k, E)
        lo, n = PARTS[part]
        return pltpu.make_async_remote_copy(
            src_ref=G.at[to, :, pl.ds(lo, n)],
            dst_ref=X.at[core, pl.ds(pl.multiple_of(pair * BLK, BLK), BLK), pl.ds(lo, n)],
            send_sem=p3s.at[part],
            recv_sem=p3r.at[core, part],
            device_id=(r, to),
            device_id_type=MESH,
        )

    def p3_send(part):
        @pl.loop(1, E)
        def _(k):
            p3_copy(part, k).start()

        lo, n = PARTS[part]
        X[core, pl.ds(pl.multiple_of(pair * BLK, BLK), BLK), lo:lo + n] = G[i, :, lo:lo + n]

    def p3_sent(part):
        lo, n = PARTS[part]
        return pltpu.make_async_remote_copy(
            src_ref=G.at[pl.ds(0, E - 1), :, pl.ds(lo, n)],
            dst_ref=G.at[pl.ds(0, E - 1), :, pl.ds(lo, n)],
            send_sem=p3s.at[part],
            recv_sem=p3r.at[0, part],
            device_id=(r, lax.rem(i + 1, E)),
            device_id_type=MESH,
        )

    def p3_rows(h, part, rows):
        lo, n = PARTS[part]
        return pltpu.make_async_remote_copy(
            src_ref=X.at[h, pl.ds(0, rows), pl.ds(lo, n)],
            dst_ref=X.at[h, pl.ds(0, rows), pl.ds(lo, n)],
            send_sem=p3s.at[part],
            recv_sem=p3r.at[h, part],
            device_id=(r, lax.rem(i + 1, E)),
            device_id_type=MESH,
        )

    def p3_wait(h):
        for part in range(NP):
            @pl.when(core == h)
            def _():
                p3_rows(h, part, ROWS - BLK).wait_recv()

            @pl.when(core != h)
            def _():
                p3_rows(h, part, ROWS).wait_recv()

    def p8_copy(h, p, zh):
        return pltpu.make_async_remote_copy(
            src_ref=OUT.at[h, pl.ds(pl.multiple_of(p * BLK + zh * HALF, HALF), HALF)],
            dst_ref=B.at[h, i],
            send_sem=p8s.at[h],
            recv_sem=p8r.at[h],
            device_id=(r, 2 * p + (h if zh == 0 else 1 - h)),
            device_id_type=MESH,
        )

    def p8_wait(h):
        pltpu.make_async_remote_copy(
            src_ref=B.at[h, pl.ds(0, E - 1)],
            dst_ref=B.at[h, pl.ds(0, E - 1)],
            send_sem=p8s.at[h],
            recv_sem=p8r.at[h],
            device_id=(r, sib),
            device_id_type=MESH,
        ).wait_recv()

    def p8_sent(h):
        most = pl.ds(0, (E - 1) * HALF)
        return pltpu.make_async_remote_copy(
            src_ref=OUT.at[h, most],
            dst_ref=OUT.at[h, most],
            send_sem=p8s.at[h],
            recv_sem=p8r.at[h],
            device_id=(r, sib),
            device_id_type=MESH,
        )

    def group(owner):
        return lax.rem(owner + i, Z)

    def chunk(owner):
        return pl.ds(pl.multiple_of(group(owner) * CH, CH), CH)

    def piece(owner, sub):
        return pl.ds(pl.multiple_of(group(owner) * CH + sub * SUB, SUB), SUB)

    def up(h, owner):
        at = chunk(owner)

        @pl.loop(0, 4)
        def _(n):
            cols = pl.ds(pl.multiple_of(n * 512, 512), 512)
            PRE[h, at, cols] = jnp.dot(X[h, at, :], W[:, cols], preferred_element_type=jnp.float32)

    def up_two(h, first, second):
        one, two = chunk(first), chunk(second)

        @pl.loop(0, 4)
        def _(n):
            cols = pl.ds(pl.multiple_of(n * 512, 512), 512)
            rows = jnp.concatenate([X[h, one, :], X[h, two, :]], axis=0)
            got = jnp.dot(rows, W[:, cols], preferred_element_type=jnp.float32)
            PRE[h, one, cols] = got[:CH]
            PRE[h, two, cols] = got[CH:]

    def up_part(h, q):
        @pl.loop(2 * q, 2 * q + 2)
        def _(n):
            cols = pl.ds(pl.multiple_of(n * 256, 256), 256)
            PRE[h, :, cols] = jnp.dot(X[h], W[:, cols], preferred_element_type=jnp.float32)

    def down(h, owner):
        at = chunk(owner)
        OUT[h, at, :] = jnp.dot(HD[h, at, :], DN[...], preferred_element_type=jnp.float32).astype(jnp.bfloat16)
        for j in range(CH // BLK):
            p = group(owner) * (CH // BLK) + j
            for zh in range(2):
                to = 2 * p + (h if zh == 0 else 1 - h)

                @pl.when(to != i)
                def _():
                    p8_copy(h, p, zh).start()

                @pl.when(to == i)
                def _():
                    B[h, i] = OUT[h, pl.ds(pl.multiple_of(pair * BLK + zh * HALF, HALF), HALF), :]

    def rs_copy(h, way, sub, d):
        step = 1 if way == 0 else -1
        return pltpu.make_async_remote_copy(
            src_ref=RSS.at[h, way, sub, d - 1],
            dst_ref=RSR.at[h, way, sub, d - 1],
            send_sem=rss.at[h, way, sub, d - 1],
            recv_sem=rsr.at[h, way, sub, d - 1],
            device_id=(zdev(step), i),
            device_id_type=MESH,
        )

    def decode(h, way, sub, d):
        at = (h, way, sub, d - 1)
        expo = RSR[at + (TILES - 1,)].astype(jnp.float32)
        expo = jnp.concatenate([expo[:, 0:1], expo[:, 64:65]], axis=0)
        scale = jnp.broadcast_to(jnp.exp2(expo) * (1.0 / LEVELS), (SUB, 128))
        return jnp.concatenate(
            [
                RSR[at + (slice(2 * c, 2 * c + 2),)].reshape(SUB, 128).astype(jnp.float32) * scale
                for c in range(LANES)
            ],
            axis=1,
        )

    def rs_send(h, way, sub, d):
        owner = zdev(d if way == 0 else -d)
        far = FAR[h][way]
        s = PRE[h, piece(owner, sub), :]
        if d < far:
            rs_copy(h, way, sub, d + 1).wait_recv()
            s = s + decode(h, way, sub, d + 1)
        most = jnp.maximum(jnp.max(jnp.abs(s), axis=1, keepdims=True), 1e-30)
        expo = jnp.ceil(jnp.log2(most))
        code = jnp.round(s * (jnp.exp2(-expo) * LEVELS))
        code = code.astype(jnp.int32).astype(jnp.int16)
        for c in range(LANES):
            RSS[h, way, sub, d - 1, 2 * c:2 * c + 2] = code[:, c * 128:(c + 1) * 128].reshape(2, 16, 128)
        wide = jnp.broadcast_to(expo, (SUB, 128))
        low = lax.broadcasted_iota(jnp.int32, (16, 128), 1) < 64
        RSS[h, way, sub, d - 1, TILES - 1] = jnp.where(low, wide[:16], wide[16:]).astype(jnp.int32).astype(jnp.int16)
        rs_copy(h, way, sub, d).start()

    def ag_copy(h, way, sub, k):
        step = 1 if way == 0 else -1
        origin = zdev(-(k - 1) * step)
        at = piece(origin, sub)
        return pltpu.make_async_remote_copy(
            src_ref=HD.at[h, at],
            dst_ref=HD.at[h, at],
            send_sem=ags.at[h, way, sub, k - 1],
            recv_sem=agr.at[h, way, sub, k - 1],
            device_id=(zdev(step), i),
            device_id_type=MESH,
        )

    def ag_wait(h, way, sub, k):
        step = 1 if way == 0 else -1
        origin = zdev(-k * step)
        at = piece(origin, sub)
        pltpu.make_async_remote_copy(
            src_ref=HD.at[h, at],
            dst_ref=HD.at[h, at],
            send_sem=ags.at[h, way, sub, k - 1],
            recv_sem=agr.at[h, way, sub, k - 1],
            device_id=(zdev(step), i),
            device_id_type=MESH,
        ).wait_recv()

    def finish(h, sub):
        at = piece(r, sub)
        s = PRE[h, at, :]
        for way in range(2):
            rs_copy(h, way, sub, 1).wait_recv()
            s = s + decode(h, way, sub, 1)
        g = s[:, :FF]
        HD[h, at, :] = (g / (1.0 + jnp.exp(-g)) * s[:, FF:]).astype(jnp.bfloat16)
        for way in range(2):
            ag_copy(h, way, sub, 1).start()

    def ag_step(h, way, sub, k):
        ag_wait(h, way, sub, k)
        if k < FAR[h][way]:
            ag_copy(h, way, sub, k + 1).start()

    def whose(h):
        return lax.rem(core + h, 2)

    def combine(h):
        CB[h] = lax.dot_general(
            CT[whose(h)], B[h].reshape(ROWS, DS), (((0,), (0,)), ((), ())), preferred_element_type=jnp.float32
        ).astype(jnp.bfloat16)

    mine = pl.ds(pl.multiple_of(r * DS, 128), DS)

    def p10_copy(h, q, part):
        w = whose(h)
        cl = lax.rem(q + r // 2, 4)
        lo, n = PARTS[part]
        return pltpu.make_async_remote_copy(
            src_ref=CB.at[h, pl.ds(pl.multiple_of(cl * TOK, TOK), TOK), pl.ds(lo, n)],
            dst_ref=comb_out.at[:, pl.ds(pl.multiple_of(r * DS + lo, 128), n)],
            send_sem=p10s.at[h, cl],
            recv_sem=p10r.at[r],
            device_id=(2 * cl + w, i + w * (sib - i)),
            device_id_type=MESH,
        )

    def p10_away(h, q):
        w = whose(h)
        cl = lax.rem(q + r // 2, 4)
        return jnp.logical_or(w == 1, 2 * cl + w != r)

    def p10_self():
        return pltpu.make_async_copy(
            CB.at[core, pl.ds(pl.multiple_of((r // 2) * TOK, TOK), TOK)], comb_out.at[:, mine], loc.at[3]
        )

    def p10_send(h, first, last):
        for q, part in PIECES[first:last]:
            @pl.when(p10_away(h, q))
            def _():
                p10_copy(h, q, part).start()

    def hessian():
        at = pl.ds(pl.multiple_of(r * 128, 128), 128)
        total = lax.dot_general(
            HD[0, :, at], HD[0], (((0,), (0,)), ((), ())), preferred_element_type=jnp.float32
        ) + lax.dot_general(
            HD[1, :, at], HD[1], (((0,), (0,)), ((), ())), preferred_element_type=jnp.float32
        )
        hess_out[...] = total * (2.0 / 1024.0)

    def layout(first, last):
        @pl.loop(first, last)
        def _(n):
            at = pl.ds(pl.multiple_of(n * 64, 64), 64)
            W[at, :FF] = W3V[at, 0, :]
            W[at, FF:] = W3V[at, 1, :]

    def ag(h, k, sub):
        for way in range(2):
            if k <= FAR[h][way]:
                ag_step(h, way, sub, k)

    def downs(h, k):
        for way in range(2):
            if k <= FAR[h][way]:
                down(h, zdev(-k if way == 0 else k))

    def hand_in(part, h):
        @pl.when(core == h)
        def _():
            p1_wait(part)
            gather(part)
            if h == 0:
                p3_send(part)

    def hand_out(h):
        p8_wait(h)
        combine(h)

        @pl.when(jnp.logical_and(core == h, lax.rem(r, 2) == 0))
        def _():
            p10_self().start()

    meta_send()

    @pl.when(core == 0)
    def _():
        p1_send()

    w_copy.wait()
    layout(0, 8)
    own_copy.wait()
    meta_wait()
    routes()
    hand_in(0, 0)
    hand_in(1, 0)

    @pl.when(core == 0)
    def _():
        pl.semaphore_signal(go, inc=1, device_id=(r, i + 1), device_id_type=MESH)

    @pl.when(core == 1)
    def _():
        pl.semaphore_wait(go, 1)
        p1_send()

    for part in range(2, NP):
        hand_in(part, 0)
    returns()
    layout(8, 14)
    for part in range(NP - 1):
        hand_in(part, 1)
    p3_wait(0)

    @pl.when(core == 1)
    def _():
        for part in range(NP - 1):
            p3_send(part)

    up_two(0, zdev(4), zdev(-3))
    for sub in range(NSUB):
        rs_send(0, 0, sub, 4)
        rs_send(0, 1, sub, 3)
    hand_in(NP - 1, 1)

    @pl.when(core == 1)
    def _():
        p3_send(NP - 1)

    for q in range(4):
        up_part(0, q)
    for d in (3, 2):
        for sub in range(NSUB):
            rs_send(0, 0, sub, d)
            rs_send(0, 1, sub, d - 1)
    dn_copy.wait()
    p3_wait(1)
    up(1, zdev(-4))
    for sub in range(NSUB):
        rs_send(1, 1, sub, 4)
        rs_send(0, 0, sub, 1)
    for q in range(4):
        up_part(1, q)
    for sub in range(NSUB):
        finish(0, sub)
        rs_send(1, 0, sub, 3)
        rs_send(1, 1, sub, 3)
    down(0, r)
    ag(0, 1, 0)
    rs_send(1, 0, 0, 2)
    rs_send(1, 1, 0, 2)
    ag(0, 1, 1)
    ag(0, 2, 0)
    downs(0, 1)
    rs_send(1, 0, 1, 2)
    rs_send(1, 1, 1, 2)
    ag(0, 2, 1)
    ag(0, 3, 0)
    downs(0, 2)
    rs_send(1, 0, 0, 1)
    rs_send(1, 1, 0, 1)
    ag(0, 3, 1)
    ag(0, 4, 0)
    downs(0, 3)
    rs_send(1, 0, 1, 1)
    rs_send(1, 1, 1, 1)
    ag(0, 4, 1)
    downs(0, 4)
    for sub in range(NSUB):
        finish(1, sub)
    down(1, r)
    for sub in range(NSUB):
        ag(1, 1, sub)
    downs(1, 1)
    ag(1, 2, 0)
    ag(1, 2, 1)
    downs(1, 2)
    ag(1, 3, 0)
    ag(1, 3, 1)
    hand_out(0)
    p10_send(0, 0, 6)
    downs(1, 3)
    for sub in range(NSUB):
        ag(1, 4, sub)
    downs(1, 4)
    p10_send(0, 6, 16)
    hessian()
    hand_out(1)
    p10_send(1, 0, 16)

    @pl.loop(1, Z)
    def _(k):
        for part in range(NP):
            tok_copy(k, part).wait_send()
        meta_copy(k).wait_send()

    sib_copy.wait_send()
    for part in range(NP):
        p3_sent(part).wait_send()

    for h in range(2):
        p8_sent(h).wait_send()
        for way in range(2):
            for sub in range(NSUB):
                for d in range(1, FAR[h][way] + 1):
                    rs_copy(h, way, sub, d).wait_send()
                    ag_copy(h, way, sub, d).wait_send()
        for q in range(4):
            cl = lax.rem(q + r // 2, 4)

            @pl.when(p10_away(h, q))
            def _():
                pltpu.make_async_remote_copy(
                    src_ref=CB.at[h, pl.ds(pl.multiple_of(cl * TOK, TOK), TOK)],
                    dst_ref=comb_out.at[:, mine],
                    send_sem=p10s.at[h, cl],
                    recv_sem=p10r.at[r],
                    device_id=(r, sib),
                    device_id_type=MESH,
                ).wait_send()

    @pl.when(lax.rem(r, 2) == 0)
    def _():
        p10_self().wait()

    @pl.loop(0, Z)
    def _(k):
        c = zdev(k)

        @pl.when(jnp.logical_or(lax.rem(r, 2) == 1, k != 0))
        def _():
            pltpu.make_async_remote_copy(
                src_ref=CB.at[0, pl.ds(0, TOK)],
                dst_ref=comb_out.at[:, pl.ds(pl.multiple_of(c * DS, 128), DS)],
                send_sem=p10s.at[0, 0],
                recv_sem=p10r.at[c],
                device_id=(r, sib),
                device_id_type=MESH,
            ).wait_recv()


def local(tokens, expert_ids, combine_weights, gate_up_weight, down_weight):
    bf, f32 = jnp.bfloat16, jnp.float32
    dma = pltpu.SemaphoreType.DMA
    comb, hess = pl.pallas_call(
        kernel,
        out_shape=(
            jax.ShapeDtypeStruct((TOK, D), bf),
            jax.ShapeDtypeStruct((128, FF), f32),
        ),
        in_specs=[
            pl.BlockSpec(memory_space=pl.ANY),
            pl.BlockSpec(memory_space=pltpu.VMEM),
            pl.BlockSpec(memory_space=pltpu.VMEM),
            pl.BlockSpec(memory_space=pl.ANY),
            pl.BlockSpec(memory_space=pl.ANY),
        ],
        out_specs=(
            pl.BlockSpec(memory_space=pl.ANY),
            pl.BlockSpec(memory_space=pltpu.VMEM),
        ),
        scratch_shapes=[
            pltpu.VMEM((8, 128), f32),
            pltpu.VMEM((2, 4 * TOK, DS), bf),
            pltpu.VMEM((2, 4, 8, 128), f32),
            pltpu.VMEM((4, 8, 128), f32),
            pltpu.VMEM((2, ROWS, 4 * TOK), bf),
            pltpu.VMEM((2, ROWS, 4 * TOK), bf),
            pltpu.VMEM((E, BLK, DS), bf),
            pltpu.VMEM((2, ROWS, DS), bf),
            pltpu.VMEM((DS, 2, FF), bf),
            pltpu.VMEM((DS, 2 * FF), bf),
            pltpu.VMEM((FF, DS), bf),
            pltpu.VMEM((2, ROWS, 2 * FF), f32),
            pltpu.VMEM((2, 2, NSUB, 4, TILES, 16, 128), jnp.int16),
            pltpu.VMEM((2, 2, NSUB, 4, TILES, 16, 128), jnp.int16),
            pltpu.VMEM((2, ROWS, FF), bf),
            pltpu.VMEM((2, ROWS, DS), bf),
            pltpu.VMEM((2, E, HALF, DS), bf),
            pltpu.VMEM((2, 4 * TOK, DS), bf),
            pltpu.SemaphoreType.REGULAR,
            dma,
            dma,
            dma((4,)),
            dma((Z, NP)),
            dma((Z, NP)),
            dma((Z,)),
            dma((Z,)),
            dma((NP,)),
            dma((2, NP)),
            dma((2, 2, NSUB, 4)),
            dma((2, 2, NSUB, 4)),
            dma((2, 2, NSUB, 4)),
            dma((2, 2, NSUB, 4)),
            dma((2,)),
            dma((2,)),
            dma((2, 4)),
            dma((Z,)),
        ],
        compiler_params=pltpu.CompilerParams(
            collective_id=0, has_side_effects=True, vmem_limit_bytes=60 * 1024 * 1024
        ),
        name="moe",
    )(tokens, expert_ids.T, combine_weights.T, gate_up_weight[0], down_weight[0])
    return comb.astype(jnp.float32), hess[None]


def solution(mesh):
    return jax.shard_map(
        local,
        mesh=mesh,
        in_specs=(
            P(("rep", "exp"), None),
            P(("rep", "exp"), None),
            P(("rep", "exp"), None),
            P("exp", "rep", None, None),
            P("exp", None, "rep"),
        ),
        out_specs=(P(("rep", "exp"), None), P("exp", "rep", None)),
        check_vma=False,
    )
```

```python
import functools

import jax
import jax.numpy as jnp
from jax import lax
from jax.experimental import pallas as pl
from jax.experimental.pallas import tpu as pltpu
from jax.sharding import PartitionSpec as P

MESH = pl.DeviceIdType.MESH
Z = 8
E = 32
TOK = 64
SLOT = 4
D = 7168
DS = D // Z
FF = 1024
ROWS = 512
HALF = 16
BLK = 32
CH = ROWS // Z
NSUB = 2
SUB = CH // NSUB
LANES = 2 * FF // 128
TILES = 2 * LANES + 1
LEVELS = 32000.0
FAR = ((4, 3), (3, 4))
PARTS = ((0, 128), (128, 256), (384, 256), (640, 256))
NP = len(PARTS)
PIECES = [(q, part) for part in range(NP) for q in range(4)]


def kernel(
    tok, ids, wts, w3, dn, comb_out, hess_out,
    META, T, M, MS, DM, CT, G, X, W3V, W, DN, PRE, RSS, RSR, HD, OUT, B, CB,
    go, sibs, sibr, loc, p1s, p1r, m1s, m1r, p3s, p3r, rss, rsr, ags, agr, p8s, p8r, p10s, p10r,
):
    r = lax.axis_index("rep")
    i = lax.axis_index("exp")
    core = lax.rem(i, 2)
    pair = i // 2
    sib = i + 1 - 2 * core
    zh_own, cl_own = lax.rem(r, 2), r // 2

    def zdev(k):
        return lax.rem(r + k + Z, Z)

    w_copy = pltpu.make_async_copy(w3, W3V, loc.at[0])
    dn_copy = pltpu.make_async_copy(dn, DN, loc.at[1])
    own_copy = pltpu.make_async_copy(
        tok.at[:, pl.ds(pl.multiple_of(r * DS, 128), DS)],
        T.at[zh_own, pl.ds(pl.multiple_of(cl_own * TOK, TOK), TOK)],
        loc.at[2],
    )
    own_copy.start()
    w_copy.start()
    dn_copy.start()

    barrier = pltpu.get_barrier_semaphore()

    @pl.loop(1, Z)
    def _(k):
        pl.semaphore_signal(barrier, inc=1, device_id=(zdev(k), i), device_id_type=MESH)
        pl.semaphore_signal(barrier, inc=1, device_id=(zdev(k), sib), device_id_type=MESH)

    @pl.loop(1, E)
    def _(k):
        pl.semaphore_signal(barrier, inc=1, device_id=(r, lax.rem(i + k, E)), device_id_type=MESH)

    pl.semaphore_wait(barrier, 2 * (Z - 1) + E - 1)

    def tok_copy(k, part):
        to = zdev(k)
        lo, n = PARTS[part]
        return pltpu.make_async_remote_copy(
            src_ref=tok.at[:, pl.ds(pl.multiple_of(to * DS + lo, 128), n)],
            dst_ref=T.at[zh_own, pl.ds(pl.multiple_of(cl_own * TOK, TOK), TOK), pl.ds(lo, n)],
            send_sem=p1s.at[k, part],
            recv_sem=p1r.at[r, part],
            device_id=(to, i),
            device_id_type=MESH,
        )

    def meta_copy(k):
        return pltpu.make_async_remote_copy(
            src_ref=META,
            dst_ref=M.at[zh_own, cl_own],
            send_sem=m1s.at[k],
            recv_sem=m1r.at[r],
            device_id=(zdev(k), i),
            device_id_type=MESH,
        )

    def p1_send():
        for part in range(NP):
            @pl.loop(1, Z)
            def _(k):
                tok_copy(k, part).start()

    def meta_send():
        row = ids[...].astype(jnp.float32)
        row = jnp.concatenate([row[0:1, :], row[1:2, :]], axis=1)
        hot = lax.broadcasted_iota(jnp.int32, (E, 2 * TOK), 0).astype(jnp.float32) == row
        hot = jnp.where(hot, 1.0, 0.0)
        earlier = lax.broadcasted_iota(jnp.int32, (2 * TOK, 2 * TOK), 0) < lax.broadcasted_iota(
            jnp.int32, (2 * TOK, 2 * TOK), 1
        )
        count = jnp.dot(
            hot.astype(jnp.bfloat16),
            jnp.where(earlier, 1.0, 0.0).astype(jnp.bfloat16),
            preferred_element_type=jnp.float32,
        )
        rank = jnp.sum(hot * count, axis=0, keepdims=True)
        pos = row * HALF + rank + (cl_own * SLOT).astype(jnp.float32)
        w = wts[...].astype(jnp.float32)
        four = jnp.concatenate([pos[:, :TOK], pos[:, TOK:], w], axis=0)
        fill = jnp.where(lax.broadcasted_iota(jnp.int32, (4, TOK), 0) < 2, -1.0, 0.0)
        wide = jnp.where(
            lax.rem(cl_own, 2) == 0,
            jnp.concatenate([four, fill], axis=1),
            jnp.concatenate([fill, four], axis=1),
        )
        META[...] = jnp.concatenate([wide, wide], axis=0)
        M[zh_own, cl_own] = jnp.concatenate([wide, wide], axis=0)

        @pl.loop(1, Z)
        def _(k):
            meta_copy(k).start()

    def meta_wait():
        @pl.loop(1, Z)
        def _(k):
            c = zdev(k)
            pltpu.make_async_remote_copy(
                src_ref=META,
                dst_ref=M.at[lax.rem(c, 2), c // 2],
                send_sem=m1s.at[k],
                recv_sem=m1r.at[c],
                device_id=(c, i),
                device_id_type=MESH,
            ).wait_recv()

    def p1_wait(part):
        lo, n = PARTS[part]

        @pl.loop(1, Z)
        def _(k):
            c = zdev(k)
            at = pl.ds(pl.multiple_of((c // 2) * TOK, TOK), TOK)
            zh = lax.rem(c, 2)
            pltpu.make_async_remote_copy(
                src_ref=T.at[zh, at, pl.ds(lo, n)],
                dst_ref=T.at[zh, at, pl.ds(lo, n)],
                send_sem=p1s.at[k, part],
                recv_sem=p1r.at[c, part],
                device_id=(c, i),
                device_id_type=MESH,
            ).wait_recv()

    sib_copy = pltpu.make_async_remote_copy(
        src_ref=M.at[1], dst_ref=MS, send_sem=sibs, recv_sem=sibr, device_id=(r, sib), device_id_type=MESH
    )

    def hits(m):
        rows = lax.broadcasted_iota(jnp.int32, (ROWS, 128), 0).astype(jnp.float32)
        return rows == m[0:1, :], rows == m[1:2, :]

    def weights(which, p, m):
        hit0, hit1 = hits(m)
        CT[which, :, p * 128:(p + 1) * 128] = (
            jnp.where(hit0, m[2:3, :], 0.0) + jnp.where(hit1, m[3:4, :], 0.0)
        ).astype(jnp.bfloat16)

    def routes():
        sib_copy.start()
        for p in range(2):
            for zh in range(2):
                m = jnp.maximum(M[zh, 2 * p], M[zh, 2 * p + 1])
                hit0, hit1 = hits(m)
                DM[zh, :, p * 128:(p + 1) * 128] = jnp.where(hit0 | hit1, 1.0, 0.0).astype(jnp.bfloat16)

    def returns():
        sib_copy.wait_recv()
        for p in range(2):
            weights(0, p, jnp.maximum(M[0, 2 * p], M[0, 2 * p + 1]))
            weights(1, p, jnp.maximum(MS[2 * p], MS[2 * p + 1]))

    def gather(part):
        lo, n = PARTS[part]
        for zh in range(2):
            @pl.loop(0, 4)
            def _(q):
                at = pl.ds(pl.multiple_of(q * 128, 128), 128)
                got = jnp.dot(DM[zh, at, :], T[zh, :, lo:lo + n], preferred_element_type=jnp.float32)
                G[pl.ds(q * 8, 8), zh * HALF:(zh + 1) * HALF, lo:lo + n] = got.astype(jnp.bfloat16).reshape(8, HALF, n)

    def p3_copy(part, k):
        to = lax.rem(i + k, E)
        lo, n = PARTS[part]
        return pltpu.make_async_remote_copy(
            src_ref=G.at[to, :, pl.ds(lo, n)],
            dst_ref=X.at[core, pl.ds(pl.multiple_of(pair * BLK, BLK), BLK), pl.ds(lo, n)],
            send_sem=p3s.at[part],
            recv_sem=p3r.at[core, part],
            device_id=(r, to),
            device_id_type=MESH,
        )

    def p3_send(part):
        @pl.loop(1, E)
        def _(k):
            p3_copy(part, k).start()

        lo, n = PARTS[part]
        X[core, pl.ds(pl.multiple_of(pair * BLK, BLK), BLK), lo:lo + n] = G[i, :, lo:lo + n]

    def p3_sent(part):
        lo, n = PARTS[part]
        return pltpu.make_async_remote_copy(
            src_ref=G.at[pl.ds(0, E - 1), :, pl.ds(lo, n)],
            dst_ref=G.at[pl.ds(0, E - 1), :, pl.ds(lo, n)],
            send_sem=p3s.at[part],
            recv_sem=p3r.at[0, part],
            device_id=(r, lax.rem(i + 1, E)),
            device_id_type=MESH,
        )

    def p3_rows(h, part, rows):
        lo, n = PARTS[part]
        return pltpu.make_async_remote_copy(
            src_ref=X.at[h, pl.ds(0, rows), pl.ds(lo, n)],
            dst_ref=X.at[h, pl.ds(0, rows), pl.ds(lo, n)],
            send_sem=p3s.at[part],
            recv_sem=p3r.at[h, part],
            device_id=(r, lax.rem(i + 1, E)),
            device_id_type=MESH,
        )

    def p3_wait(h):
        for part in range(NP):
            @pl.when(core == h)
            def _():
                p3_rows(h, part, ROWS - BLK).wait_recv()

            @pl.when(core != h)
            def _():
                p3_rows(h, part, ROWS).wait_recv()

    def p8_copy(h, p, zh):
        return pltpu.make_async_remote_copy(
            src_ref=OUT.at[h, pl.ds(pl.multiple_of(p * BLK + zh * HALF, HALF), HALF)],
            dst_ref=B.at[h, i],
            send_sem=p8s.at[h],
            recv_sem=p8r.at[h],
            device_id=(r, 2 * p + (h if zh == 0 else 1 - h)),
            device_id_type=MESH,
        )

    def p8_wait(h):
        pltpu.make_async_remote_copy(
            src_ref=B.at[h, pl.ds(0, E - 1)],
            dst_ref=B.at[h, pl.ds(0, E - 1)],
            send_sem=p8s.at[h],
            recv_sem=p8r.at[h],
            device_id=(r, sib),
            device_id_type=MESH,
        ).wait_recv()

    def p8_sent(h):
        most = pl.ds(0, (E - 1) * HALF)
        return pltpu.make_async_remote_copy(
            src_ref=OUT.at[h, most],
            dst_ref=OUT.at[h, most],
            send_sem=p8s.at[h],
            recv_sem=p8r.at[h],
            device_id=(r, sib),
            device_id_type=MESH,
        )

    def group(owner):
        return lax.rem(owner + i, Z)

    def chunk(owner):
        return pl.ds(pl.multiple_of(group(owner) * CH, CH), CH)

    def piece(owner, sub):
        return pl.ds(pl.multiple_of(group(owner) * CH + sub * SUB, SUB), SUB)

    def up(h, owner):
        at = chunk(owner)

        @pl.loop(0, 4)
        def _(n):
            cols = pl.ds(pl.multiple_of(n * 512, 512), 512)
            PRE[h, at, cols] = jnp.dot(X[h, at, :], W[:, cols], preferred_element_type=jnp.float32)

    def up_two(h, first, second):
        one, two = chunk(first), chunk(second)

        @pl.loop(0, 4)
        def _(n):
            cols = pl.ds(pl.multiple_of(n * 512, 512), 512)
            rows = jnp.concatenate([X[h, one, :], X[h, two, :]], axis=0)
            got = jnp.dot(rows, W[:, cols], preferred_element_type=jnp.float32)
            PRE[h, one, cols] = got[:CH]
            PRE[h, two, cols] = got[CH:]

    def up_part(h, q):
        @pl.loop(2 * q, 2 * q + 2)
        def _(n):
            cols = pl.ds(pl.multiple_of(n * 256, 256), 256)
            PRE[h, :, cols] = jnp.dot(X[h], W[:, cols], preferred_element_type=jnp.float32)

    def down(h, owner):
        at = chunk(owner)
        OUT[h, at, :] = jnp.dot(HD[h, at, :], DN[...], preferred_element_type=jnp.float32).astype(jnp.bfloat16)
        for j in range(CH // BLK):
            p = group(owner) * (CH // BLK) + j
            for zh in range(2):
                to = 2 * p + (h if zh == 0 else 1 - h)

                @pl.when(to != i)
                def _():
                    p8_copy(h, p, zh).start()

                @pl.when(to == i)
                def _():
                    B[h, i] = OUT[h, pl.ds(pl.multiple_of(pair * BLK + zh * HALF, HALF), HALF), :]

    def rs_copy(h, way, sub, d):
        step = 1 if way == 0 else -1
        return pltpu.make_async_remote_copy(
            src_ref=RSS.at[h, way, sub, d - 1],
            dst_ref=RSR.at[h, way, sub, d - 1],
            send_sem=rss.at[h, way, sub, d - 1],
            recv_sem=rsr.at[h, way, sub, d - 1],
            device_id=(zdev(step), i),
            device_id_type=MESH,
        )

    def decode(h, way, sub, d):
        at = (h, way, sub, d - 1)
        expo = RSR[at + (TILES - 1,)].astype(jnp.float32)
        expo = jnp.concatenate([expo[:, 0:1], expo[:, 64:65]], axis=0)
        scale = jnp.broadcast_to(jnp.exp2(expo) * (1.0 / LEVELS), (SUB, 128))
        return jnp.concatenate(
            [
                RSR[at + (slice(2 * c, 2 * c + 2),)].reshape(SUB, 128).astype(jnp.float32) * scale
                for c in range(LANES)
            ],
            axis=1,
        )

    def rs_send(h, way, sub, d):
        owner = zdev(d if way == 0 else -d)
        far = FAR[h][way]
        s = PRE[h, piece(owner, sub), :]
        if d < far:
            rs_copy(h, way, sub, d + 1).wait_recv()
            s = s + decode(h, way, sub, d + 1)
        most = jnp.maximum(jnp.max(jnp.abs(s), axis=1, keepdims=True), 1e-30)
        expo = jnp.ceil(jnp.log2(most))
        code = jnp.round(s * (jnp.exp2(-expo) * LEVELS))
        code = code.astype(jnp.int32).astype(jnp.int16)
        for c in range(LANES):
            RSS[h, way, sub, d - 1, 2 * c:2 * c + 2] = code[:, c * 128:(c + 1) * 128].reshape(2, 16, 128)
        wide = jnp.broadcast_to(expo, (SUB, 128))
        low = lax.broadcasted_iota(jnp.int32, (16, 128), 1) < 64
        RSS[h, way, sub, d - 1, TILES - 1] = jnp.where(low, wide[:16], wide[16:]).astype(jnp.int32).astype(jnp.int16)
        rs_copy(h, way, sub, d).start()

    def ag_copy(h, way, sub, k):
        step = 1 if way == 0 else -1
        origin = zdev(-(k - 1) * step)
        at = piece(origin, sub)
        return pltpu.make_async_remote_copy(
            src_ref=HD.at[h, at],
            dst_ref=HD.at[h, at],
            send_sem=ags.at[h, way, sub, k - 1],
            recv_sem=agr.at[h, way, sub, k - 1],
            device_id=(zdev(step), i),
            device_id_type=MESH,
        )

    def ag_wait(h, way, sub, k):
        step = 1 if way == 0 else -1
        origin = zdev(-k * step)
        at = piece(origin, sub)
        pltpu.make_async_remote_copy(
            src_ref=HD.at[h, at],
            dst_ref=HD.at[h, at],
            send_sem=ags.at[h, way, sub, k - 1],
            recv_sem=agr.at[h, way, sub, k - 1],
            device_id=(zdev(step), i),
            device_id_type=MESH,
        ).wait_recv()

    def finish(h, sub):
        at = piece(r, sub)
        s = PRE[h, at, :]
        for way in range(2):
            rs_copy(h, way, sub, 1).wait_recv()
            s = s + decode(h, way, sub, 1)
        g = s[:, :FF]
        HD[h, at, :] = (g / (1.0 + jnp.exp(-g)) * s[:, FF:]).astype(jnp.bfloat16)
        for way in range(2):
            ag_copy(h, way, sub, 1).start()

    def ag_step(h, way, sub, k):
        ag_wait(h, way, sub, k)
        if k < FAR[h][way]:
            ag_copy(h, way, sub, k + 1).start()

    def whose(h):
        return lax.rem(core + h, 2)

    def combine(h):
        CB[h] = lax.dot_general(
            CT[whose(h)], B[h].reshape(ROWS, DS), (((0,), (0,)), ((), ())), preferred_element_type=jnp.float32
        ).astype(jnp.bfloat16)

    mine = pl.ds(pl.multiple_of(r * DS, 128), DS)

    def p10_copy(h, q, part):
        w = whose(h)
        cl = lax.rem(q + r // 2, 4)
        lo, n = PARTS[part]
        return pltpu.make_async_remote_copy(
            src_ref=CB.at[h, pl.ds(pl.multiple_of(cl * TOK, TOK), TOK), pl.ds(lo, n)],
            dst_ref=comb_out.at[:, pl.ds(pl.multiple_of(r * DS + lo, 128), n)],
            send_sem=p10s.at[h, cl],
            recv_sem=p10r.at[r],
            device_id=(2 * cl + w, i + w * (sib - i)),
            device_id_type=MESH,
        )

    def p10_away(h, q):
        w = whose(h)
        cl = lax.rem(q + r // 2, 4)
        return jnp.logical_or(w == 1, 2 * cl + w != r)

    def p10_self():
        return pltpu.make_async_copy(
            CB.at[core, pl.ds(pl.multiple_of((r // 2) * TOK, TOK), TOK)], comb_out.at[:, mine], loc.at[3]
        )

    def p10_send(h, first, last):
        for q, part in PIECES[first:last]:
            @pl.when(p10_away(h, q))
            def _():
                p10_copy(h, q, part).start()

    def hessian():
        at = pl.ds(pl.multiple_of(r * 128, 128), 128)
        total = lax.dot_general(
            HD[0, :, at], HD[0], (((0,), (0,)), ((), ())), preferred_element_type=jnp.float32
        ) + lax.dot_general(
            HD[1, :, at], HD[1], (((0,), (0,)), ((), ())), preferred_element_type=jnp.float32
        )
        hess_out[...] = total * (2.0 / 1024.0)

    def layout(first, last):
        @pl.loop(first, last)
        def _(n):
            at = pl.ds(pl.multiple_of(n * 64, 64), 64)
            W[at, :FF] = W3V[at, 0, :]
            W[at, FF:] = W3V[at, 1, :]

    def ag(h, k, sub):
        for way in range(2):
            if k <= FAR[h][way]:
                ag_step(h, way, sub, k)

    def downs(h, k):
        for way in range(2):
            if k <= FAR[h][way]:
                down(h, zdev(-k if way == 0 else k))

    def hand_in(part, h):
        @pl.when(core == h)
        def _():
            p1_wait(part)
            gather(part)
            if h == 0:
                p3_send(part)

    def hand_out(h):
        p8_wait(h)
        combine(h)

        @pl.when(jnp.logical_and(core == h, lax.rem(r, 2) == 0))
        def _():
            p10_self().start()

    meta_send()

    @pl.when(core == 0)
    def _():
        p1_send()

    w_copy.wait()
    layout(0, 8)
    own_copy.wait()
    meta_wait()
    routes()
    hand_in(0, 0)

    @pl.when(core == 0)
    def _():
        pl.semaphore_signal(go, inc=1, device_id=(r, i + 1), device_id_type=MESH)

    @pl.when(core == 1)
    def _():
        pl.semaphore_wait(go, 1)
        p1_send()

    for part in range(1, NP):
        hand_in(part, 0)
    returns()
    layout(8, 14)
    for part in range(NP - 1):
        hand_in(part, 1)
    p3_wait(0)

    @pl.when(core == 1)
    def _():
        for part in range(NP - 1):
            p3_send(part)

    up_two(0, zdev(4), zdev(-3))
    for sub in range(NSUB):
        rs_send(0, 0, sub, 4)
        rs_send(0, 1, sub, 3)
    hand_in(NP - 1, 1)

    @pl.when(core == 1)
    def _():
        p3_send(NP - 1)

    for q in range(4):
        up_part(0, q)
    for d in (3, 2):
        for sub in range(NSUB):
            rs_send(0, 0, sub, d)
            rs_send(0, 1, sub, d - 1)
    dn_copy.wait()
    p3_wait(1)
    up(1, zdev(-4))
    for sub in range(NSUB):
        rs_send(1, 1, sub, 4)
        rs_send(0, 0, sub, 1)
    for q in range(4):
        up_part(1, q)
    for sub in range(NSUB):
        finish(0, sub)
        rs_send(1, 0, sub, 3)
        rs_send(1, 1, sub, 3)
    down(0, r)
    ag(0, 1, 0)
    rs_send(1, 0, 0, 2)
    rs_send(1, 1, 0, 2)
    ag(0, 1, 1)
    ag(0, 2, 0)
    downs(0, 1)
    rs_send(1, 0, 1, 2)
    rs_send(1, 1, 1, 2)
    ag(0, 2, 1)
    ag(0, 3, 0)
    downs(0, 2)
    rs_send(1, 0, 0, 1)
    rs_send(1, 1, 0, 1)
    ag(0, 3, 1)
    ag(0, 4, 0)
    downs(0, 3)
    rs_send(1, 0, 1, 1)
    rs_send(1, 1, 1, 1)
    ag(0, 4, 1)
    downs(0, 4)
    for sub in range(NSUB):
        finish(1, sub)
    down(1, r)
    for sub in range(NSUB):
        ag(1, 1, sub)
    downs(1, 1)
    ag(1, 2, 0)
    ag(1, 2, 1)
    downs(1, 2)
    ag(1, 3, 0)
    ag(1, 3, 1)
    hand_out(0)
    p10_send(0, 0, 6)
    downs(1, 3)
    for sub in range(NSUB):
        ag(1, 4, sub)
    downs(1, 4)
    p10_send(0, 6, 16)
    hessian()
    hand_out(1)
    p10_send(1, 0, 16)

    @pl.loop(1, Z)
    def _(k):
        for part in range(NP):
            tok_copy(k, part).wait_send()
        meta_copy(k).wait_send()

    sib_copy.wait_send()
    for part in range(NP):
        p3_sent(part).wait_send()

    for h in range(2):
        p8_sent(h).wait_send()
        for way in range(2):
            for sub in range(NSUB):
                for d in range(1, FAR[h][way] + 1):
                    rs_copy(h, way, sub, d).wait_send()
                    ag_copy(h, way, sub, d).wait_send()
        for q in range(4):
            cl = lax.rem(q + r // 2, 4)

            @pl.when(p10_away(h, q))
            def _():
                pltpu.make_async_remote_copy(
                    src_ref=CB.at[h, pl.ds(pl.multiple_of(cl * TOK, TOK), TOK)],
                    dst_ref=comb_out.at[:, mine],
                    send_sem=p10s.at[h, cl],
                    recv_sem=p10r.at[r],
                    device_id=(r, sib),
                    device_id_type=MESH,
                ).wait_send()

    @pl.when(lax.rem(r, 2) == 0)
    def _():
        p10_self().wait()

    @pl.loop(0, Z)
    def _(k):
        c = zdev(k)

        @pl.when(jnp.logical_or(lax.rem(r, 2) == 1, k != 0))
        def _():
            pltpu.make_async_remote_copy(
                src_ref=CB.at[0, pl.ds(0, TOK)],
                dst_ref=comb_out.at[:, pl.ds(pl.multiple_of(c * DS, 128), DS)],
                send_sem=p10s.at[0, 0],
                recv_sem=p10r.at[c],
                device_id=(r, sib),
                device_id_type=MESH,
            ).wait_recv()


def local(tokens, expert_ids, combine_weights, gate_up_weight, down_weight):
    bf, f32 = jnp.bfloat16, jnp.float32
    dma = pltpu.SemaphoreType.DMA
    comb, hess = pl.pallas_call(
        kernel,
        out_shape=(
            jax.ShapeDtypeStruct((TOK, D), bf),
            jax.ShapeDtypeStruct((128, FF), f32),
        ),
        in_specs=[
            pl.BlockSpec(memory_space=pl.ANY),
            pl.BlockSpec(memory_space=pltpu.VMEM),
            pl.BlockSpec(memory_space=pltpu.VMEM),
            pl.BlockSpec(memory_space=pl.ANY),
            pl.BlockSpec(memory_space=pl.ANY),
        ],
        out_specs=(
            pl.BlockSpec(memory_space=pl.ANY),
            pl.BlockSpec(memory_space=pltpu.VMEM),
        ),
        scratch_shapes=[
            pltpu.VMEM((8, 128), f32),
            pltpu.VMEM((2, 4 * TOK, DS), bf),
            pltpu.VMEM((2, 4, 8, 128), f32),
            pltpu.VMEM((4, 8, 128), f32),
            pltpu.VMEM((2, ROWS, 4 * TOK), bf),
            pltpu.VMEM((2, ROWS, 4 * TOK), bf),
            pltpu.VMEM((E, BLK, DS), bf),
            pltpu.VMEM((2, ROWS, DS), bf),
            pltpu.VMEM((DS, 2, FF), bf),
            pltpu.VMEM((DS, 2 * FF), bf),
            pltpu.VMEM((FF, DS), bf),
            pltpu.VMEM((2, ROWS, 2 * FF), f32),
            pltpu.VMEM((2, 2, NSUB, 4, TILES, 16, 128), jnp.int16),
            pltpu.VMEM((2, 2, NSUB, 4, TILES, 16, 128), jnp.int16),
            pltpu.VMEM((2, ROWS, FF), bf),
            pltpu.VMEM((2, ROWS, DS), bf),
            pltpu.VMEM((2, E, HALF, DS), bf),
            pltpu.VMEM((2, 4 * TOK, DS), bf),
            pltpu.SemaphoreType.REGULAR,
            dma,
            dma,
            dma((4,)),
            dma((Z, NP)),
            dma((Z, NP)),
            dma((Z,)),
            dma((Z,)),
            dma((NP,)),
            dma((2, NP)),
            dma((2, 2, NSUB, 4)),
            dma((2, 2, NSUB, 4)),
            dma((2, 2, NSUB, 4)),
            dma((2, 2, NSUB, 4)),
            dma((2,)),
            dma((2,)),
            dma((2, 4)),
            dma((Z,)),
        ],
        compiler_params=pltpu.CompilerParams(
            collective_id=0, has_side_effects=True, vmem_limit_bytes=60 * 1024 * 1024
        ),
        name="moe",
    )(tokens, expert_ids.T, combine_weights.T, gate_up_weight[0], down_weight[0])
    return comb.astype(jnp.float32), hess[None]


def solution(mesh):
    return jax.shard_map(
        local,
        mesh=mesh,
        in_specs=(
            P(("rep", "exp"), None),
            P(("rep", "exp"), None),
            P(("rep", "exp"), None),
            P("exp", "rep", None, None),
            P("exp", None, "rep"),
        ),
        out_specs=(P(("rep", "exp"), None), P("exp", "rep", None)),
        check_vma=False,
    )
```
